128 devices in a mesh: gx: 16 (over x, y), gy: 8 (over z, core).
Axes of the slice: x: 4, y: 4, z: 4, core: 2. Of those that a mesh axis runs over, the one named last changes fastest.
Arguments:
- enthalpy_start: float32 [8, 128, 1024], P(None, 'gx', 'gy'), may hold values from -4 to 4
- tangent_start: float32 [16, 8, 128, 1024], P(None, None, 'gx', 'gy'), may hold values from -3 to 3
- labels: int32 [8, 128, 1024], P(None, 'gx', 'gy'), may hold values 0 or 1
- curve_parameters: float32 [16], replicated, may hold values from -0.1 to 0.1
- pixel_cells: int32 [131072], P(('gx', 'gy')), may hold values from 0 to 1023, as said below
- row_slot: int32 [131072], P(('gx', 'gy')), may hold values from 0 to 131071, as said below
Outputs:
- heat_content: float32 [8, 128, 1024], P(None, 'gx', 'gy')
- tangent_end: float32 [16, 8, 128, 1024], P(None, None, 'gx', 'gy')
- jacobian: float32 [16, 131072], P(None, ('gx', 'gy'))
The draws below stay inside these ranges and needn't reach their ends.
Inputs may be any that keep to these rules, and one draw needn't show every extreme that they name: `pixel_cells`: the 1024 entries of each device's block are distinct cells of its own tile, numbered x * 128 + y within the tile. `row_slot`: A permutation of the rows; row r is owned by device r // 1024. Of one device's 1024 pixels at most 32 have rows of one owner, and every device has exactly 32 for some owner.
All inputs are finite; a program needn't handle non-finite values. No bound on the sum of `labels` on one device may be relied on, other than what follows from the above.
Results may differ from the reference program's by a relative error of at most 0.0001.
Values sent between devices are 32-bit elements; how exact they have to be, the bound alone decides.
A program may use at most 192 MiB of HBM per device.

```python
import jax
import jax.numpy as jnp

CX = 8
CY = 128
DEPTH_LAYERS = 8
COEF = 16
STEPS = 8
PIX_DEV = 1024
MOST = 32
HEAVY = 4
NX = 128
NY = 1024
PIXELS = 131072
N_GX = 16
N_GY = 8


def draw_pixel_cells(key, part):
    key = jax.random.fold_in(key, 5)
    device_keys = jax.random.split(key, N_GX * N_GY)

    def choose_cells(device_key):
        return jax.random.permutation(device_key, CX * CY)[:PIX_DEV]
    picks = jax.vmap(choose_cells)(device_keys)
    return picks.reshape(-1).astype(jnp.int32)


def draw_row_slot(key, part):
    key = jax.random.fold_in(key, 11)
    devices = N_GX * N_GY
    first_key, second_key = jax.random.split(key)
    shuffled = jax.random.permutation(first_key, devices).astype(jnp.int32)
    place_of = jnp.argsort(shuffled).astype(jnp.int32)
    values = jnp.arange(devices, dtype=jnp.int32)
    score = jnp.where(values == devices // 2, 0, jnp.where(values == devices - 1, 1, jnp.where(values == 1, 2, 3 + place_of))).astype(jnp.int32)
    offset_order = jnp.argsort(score, stable=True).astype(jnp.int32)

    def rank_pixels(device_key):
        return jax.random.permutation(device_key, PIX_DEV)
    ranks = jax.vmap(rank_pixels)(jax.random.split(second_key, devices)).astype(jnp.int32)
    group = jnp.where(ranks < HEAVY * MOST, ranks // MOST, HEAVY + (ranks - HEAVY * MOST) % (devices - HEAVY))
    owner_dev = (jnp.arange(devices, dtype=jnp.int32)[:, None] + offset_order[group]) % devices
    return (owner_dev * PIX_DEV + ranks).reshape(-1).astype(jnp.int32)


def plant(drawn, key, least, high):
    extent = drawn.shape
    spot = [jax.random.randint(jax.random.fold_in(key, axis), (), 0, extent[axis]) for axis in range(len(extent))]
    drawn = drawn.at[tuple(spot)].set(least)
    longest = extent.index(max(extent))
    spot[longest] = (spot[longest] + 1) % extent[longest]
    return drawn.at[tuple(spot)].set(high)


def steps_of(own_key, shape, pieces, low, largest):
    def one(position, shards_of):
        draws = jax.random.uniform(jax.random.fold_in(jax.random.fold_in(own_key, 6), position), (shards_of,), jnp.float32, low / len(pieces), largest / len(pieces))
        return jnp.repeat(jnp.exp(draws), shape[position] // shards_of).reshape((-1,) + (1,) * (len(shape) - position - 1))

    gain = one(*pieces[0])
    for cut in pieces[1:]:
        gain = gain * one(*cut)
    return gain


def bell_draw(key, dims, deviation, most, pieces=(), kind=jnp.bfloat16):
    array = jax.random.normal(key, dims, jnp.float32) * deviation
    if len(pieces) > 0:
        array = steps_of(key, dims, pieces, -0.22, 0.18) * array
    return jnp.clip(array, min=-most, max=most).astype(kind)


def setup_inputs(seed: int = 0) -> dict:
    key_of = jax.random.split(jax.random.key(seed), 7)
    enthalpy_start = bell_draw(key_of[0], (DEPTH_LAYERS, NX, NY), 1.0, 4.0, ((1, 16), (2, 8)), jnp.float32)
    tangent_start = bell_draw(key_of[1], (COEF, DEPTH_LAYERS, NX, NY), 0.5, 3.0, ((2, 16), (3, 8)), jnp.float32)
    labels = plant((jax.random.randint(key_of[2], (DEPTH_LAYERS, NX, NY), 0, 4) < 3).astype(jnp.int32), jax.random.fold_in(key_of[2], 1), 0, 1)
    curve_parameters = jnp.clip(jax.random.uniform(key_of[3], (COEF,), jnp.float32, -0.1, 0.1), -0.1, 0.1)
    pixel_cells = draw_pixel_cells(jax.random.fold_in(key_of[6], 71), 0)
    row_slot = draw_row_slot(jax.random.fold_in(key_of[6], 71), 0)
    return {"enthalpy_start": enthalpy_start, "tangent_start": tangent_start, "labels": labels, "curve_parameters": curve_parameters, "pixel_cells": pixel_cells, "row_slot": row_slot}


step_rate = 0.15
knot_width = 0.3


def conduction_advance(heat_content, direction_seed, melted_share, curve_parameters):
    parameter_total = curve_parameters.shape[0]
    knot_pos = -2.0 + 0.25 * (jnp.arange(parameter_total, dtype=jnp.float32) + 0.5)
    scaled = (heat_content[None] - knot_pos[:, None, None, None]) / knot_width
    kernel_shapes = jnp.exp(-scaled * scaled)
    bump_slope = -2.0 * scaled / knot_width * kernel_shapes
    scaled_kernels = curve_parameters[:, None, None, None]
    heat_level_grid = jnp.where(melted_share > 0, heat_content + jnp.sum(scaled_kernels * kernel_shapes, 0), 0.5 * heat_content)
    gradient_rate = jnp.where(melted_share > 0, 1.0 + jnp.sum(scaled_kernels * bump_slope, 0), 0.5)
    heat_level_derivative = gradient_rate[None] * direction_seed + melted_share[None] * kernel_shapes
    return heat_level_grid, heat_level_derivative


def neighbours(padded):
    return [padded[..., 2:, 1:-1, 1:-1], padded[..., :-2, 1:-1, 1:-1],
            padded[..., 1:-1, 2:, 1:-1], padded[..., 1:-1, :-2, 1:-1],
            padded[..., 1:-1, 1:-1, 2:], padded[..., 1:-1, 1:-1, :-2]]


def face_weights(conduct, padded):
    return [2.0 * conduct * other / (conduct + other) for other in neighbours(padded)]


def spread(padded, sensitivity_matrix, weights):
    net_flow = jnp.zeros_like(sensitivity_matrix)
    for weight, other in zip(weights, neighbours(padded)):
        net_flow = net_flow + weight[None] * (other - sensitivity_matrix)
    return net_flow


def reference(enthalpy_start, tangent_start, labels, curve_parameters, pixel_cells, row_slot):
    melted_share = (labels == 1).astype(jnp.float32)
    conduct = jnp.where(labels == 1, 0.5, 1.0).astype(jnp.float32)
    weights = face_weights(conduct, jnp.pad(conduct, 1))
    heat_content, direction_seed = enthalpy_start, tangent_start
    for repeat in range(STEPS):
        heat_level_grid, heat_level_derivative = conduction_advance(heat_content, direction_seed, melted_share, curve_parameters)
        sensitivity_matrix = jnp.concatenate([heat_level_grid[None], heat_level_derivative], 0)
        padded = jnp.pad(sensitivity_matrix, ((0, 0), (1, 1), (1, 1), (1, 1)))
        net_flow = spread(padded, sensitivity_matrix, weights)
        heat_content = heat_content + step_rate * net_flow[0]
        direction_seed = direction_seed + step_rate * net_flow[1:]
    heat_level_grid, heat_level_derivative = conduction_advance(heat_content, direction_seed, melted_share, curve_parameters)
    boundary_layer = heat_level_derivative[:, DEPTH_LAYERS - 1]
    device_of = jnp.arange(PIXELS, dtype=jnp.int32) // PIX_DEV
    cell_x = (device_of // N_GY) * CX + pixel_cells // CY
    cell_y = (device_of % N_GY) * CY + pixel_cells % CY
    values_at = boundary_layer[:, cell_x, cell_y]
    jacobian = jnp.zeros((COEF, PIXELS), jnp.float32).at[:, row_slot].set(values_at)
    return heat_content, direction_seed, jacobian
```

```python
import functools
import math

import jax
import jax.numpy as jnp
from jax import lax
from jax.experimental import pallas as pl
from jax.experimental.pallas import tpu as pltpu
from jax.sharding import PartitionSpec as P

STEPS = 8
COEF = 16
RATE = 0.15
WIDTH = 0.3
ROOT = math.sqrt(math.log2(math.e))
KNOTS = [-2.0 + 0.25 * (j + 0.5) for j in range(COEF)]

MAIN = 24
STRIP = 12
ALL = MAIN + STRIP
MOST = 32
MESH = pl.DeviceIdType.MESH


def lanes():
    return lax.broadcasted_iota(jnp.int32, (8, 128), 1)


def turn(v, shift, axis):
    size = v.shape[axis]
    shift = shift % size
    return v if shift == 0 else pltpu.roll(v, shift, axis)


def pack_edges(rows):
    chunk = lanes() // 8
    last = first = None
    for par in range(2):
        for x in range(8):
            at = par * 64 + x * 8
            a = turn(rows[par][x], at - 120, 1)
            b = turn(rows[par][x], at, 1)
            if last is None:
                last, first = a, b
            else:
                here = chunk == par * 8 + x
                last = jnp.where(here, a, last)
                first = jnp.where(here, b, first)
    return last, first


def build_strips(main, before, after, par):
    lane = lanes()
    block, inside = lane // 32, lane % 32
    out = []
    for g in range(STRIP):
        lo, hi = g, g + 12
        v = turn(main[lo], 8, 1)
        v = jnp.where(block == 1, turn(main[hi], 40, 1), v)
        v = jnp.where(block == 2, turn(main[lo], 80, 1), v)
        v = jnp.where(block == 3, turn(main[hi], 112, 1), v)
        for b, i in ((0, lo), (1, hi)):
            start = par * 64 + (i % 8) * 8
            left = turn(before[i // 8], b * 32 - start, 1)
            v = jnp.where((block == b) & (inside < 8), left, v)
            right = turn(after[i // 8], 64 + b * 32 + 16 - start, 1)
            v = jnp.where((block == b + 2) & (inside >= 16), right, v)
        out.append(v)
    return out


def merge(main, strips):
    lane = lanes()
    out = []
    for x in range(8):
        i = x + 8
        b, g = (0, i) if i < 12 else (1, i - 12)
        v = jnp.where(lane < 8, turn(strips[g], -(b * 32 + 8), 1), main[i])
        v = jnp.where(lane >= 120, turn(strips[g], 120 - (64 + b * 32 + 8), 1), v)
        out.append(v)
    return out


def advance(step, state, temp, wx, wy, wz):
    new = list(state)

    def own(i, t):
        fy = wy(i) * (turn(t, -1, 1) - t)
        fz = wz(i) * (turn(t, -1, 0) - t)
        return (fy - turn(fy, 1, 1)) + (fz - turn(fz, 1, 0))

    lo, hi = step, MAIN - step
    t = temp(lo)
    t_next = temp(lo + 1)
    flux = wx(lo) * (t_next - t)
    for i in range(lo + 1, hi - 1):
        t, t_next = t_next, temp(i + 1)
        below, flux = flux, wx(i) * (t_next - t)
        new[i] = state[i] + ((flux - below) + own(i, t))
    first = temp(MAIN)
    end = temp(ALL - 1)
    last_flux = wx(ALL - 1) * (turn(first, -32, 1) - end)
    below = turn(last_flux, 32, 1)
    t_next = first
    for i in range(MAIN, ALL):
        t = t_next
        if i == ALL - 1:
            flux = last_flux
        else:
            t_next = temp(i + 1) if i + 1 < ALL - 1 else end
            flux = wx(i) * (t_next - t)
        new[i] = state[i] + ((flux - below) + own(i, t))
        below = flux
    return new


def steps_kernel(
    n_gx, n_gy,
    e_ref, t_ref, lab_ref, coef_ref,
    e_out, t_out, v_out,
    el, hx_e, hx_t, pk, hp, est, tst, wst, sl, bump,
    se_sem, re_sem, st_sem, rt_sem, sp_sem, rp_sem,
):
    gx, gy = lax.axis_index("gx"), lax.axis_index("gy")

    def at(dx, dy):
        return lax.rem(gx + dx + n_gx, n_gx), lax.rem(gy + dy + n_gy, n_gy)

    around = [(dx, dy) for dx in (-1, 0, 1) for dy in (-1, 0, 1) if (dx, dy) != (0, 0)]
    barrier = pltpu.get_barrier_semaphore()
    for dx, dy in around:
        pl.semaphore_signal(barrier, inc=1, device_id=at(dx, dy), device_id_type=MESH)

    el[0:64, :] = e_ref[...]
    el[64:128, :] = jnp.where(lab_ref[...] == 1, 1.0, 0.0)
    pl.semaphore_wait(barrier, len(around))

    def send_e(d):
        return pltpu.make_async_remote_copy(
            el, hx_e.at[d], se_sem.at[d], re_sem.at[d], device_id=at(1 - 2 * d, 0), device_id_type=MESH
        )

    def send_t(q, d):
        part = pl.ds(q * 128, 128)
        return pltpu.make_async_remote_copy(
            t_ref.at[part], hx_t.at[d, part], st_sem.at[q, d], rt_sem.at[q, d],
            device_id=at(1 - 2 * d, 0), device_id_type=MESH,
        )

    def send_p(part, dx, dy):
        rows = pl.ds(0, 8) if part == 0 else pl.ds(8, 64)
        side = 0 if dy == 1 else 1
        return pltpu.make_async_remote_copy(
            pk.at[side, rows], hp.at[1 - dx, side, rows],
            sp_sem.at[part, dx + 1, side], rp_sem.at[part, 1 - dx, side],
            device_id=at(dx, dy), device_id_type=MESH,
        )

    corners = [(dx, dy) for dx in (0, -1, 1) for dy in (-1, 1)]
    for d in range(2):
        send_e(d).start()
    rows = [[el[pl.ds(par * 64 + x, 8, stride=8), :] for x in range(8)] for par in range(2)]
    last, first = pack_edges(rows)
    pk[0, 0:8, :] = last
    pk[1, 0:8, :] = first
    for dx, dy in corners:
        send_p(0, dx, dy).start()
    for q in range(2):
        for d in range(2):
            send_t(q, d).start()

    def pack_pair(q, _):
        rows = [[t_ref[pl.ds(q * 128 + par * 64 + x, 8, stride=8), :] for x in range(8)] for par in range(2)]
        last, first = pack_edges(rows)
        to = pl.ds(pl.multiple_of(8 + q * 8, 8), 8)
        pk[0, to, :] = last
        pk[1, to, :] = first
        return 0

    lax.fori_loop(0, 8, pack_pair, 0)
    for dx, dy in corners:
        send_p(1, dx, dy).start()

    def send_more(q, _):
        for d in range(2):
            send_t(q, d).start()
        return 0

    lax.fori_loop(2, 8, send_more, 0)

    for d in range(2):
        send_e(d).wait()
    for dx, dy in corners:
        send_p(0, dx, dy).wait()

    def rows_of(own, halo, base):
        got = [halo[0, pl.ds(base + x, 8, stride=8), :] for x in range(8)]
        got += [own[pl.ds(base + x, 8, stride=8), :] for x in range(8)]
        got += [halo[1, pl.ds(base + x, 8, stride=8), :] for x in range(8)]
        return got

    def strips_of(main, q, par):
        part = pl.ds(pl.multiple_of(q * 8, 8), 8)
        before = [hp[k, 0, part, :] for k in range(3)]
        after = [hp[k, 1, part, :] for k in range(3)]
        return build_strips(main, before, after, par)

    main = rows_of(el, hx_e, 64)
    pcm = main + strips_of(main, 0, 1)
    main = rows_of(el, hx_e, 0)
    start = main + strips_of(main, 0, 0)
    for i in range(ALL):
        est[i] = start[i]
        est[ALL + i] = pcm[i]

    lane = lanes()
    block, inside = lane // 32, lane % 32
    layer = lax.broadcasted_iota(jnp.int32, (8, 128), 0)
    open_x0 = jnp.where(gx == 0, 0.0, 1.0)
    open_x1 = jnp.where(gx == n_gx - 1, 0.0, 1.0)
    open_y0 = jnp.where(gy == 0, 0.0, 1.0)
    open_y1 = jnp.where(gy == n_gy - 1, 0.0, 1.0)
    cond = [1.0 - 0.5 * p for p in pcm]

    def face(a, b):
        return (2.0 * RATE) * a * b / (a + b)

    edge_y = jnp.where((block < 2) & (inside == 7), open_y0, 1.0)
    edge_y = jnp.where((block >= 2) & (inside == 15), open_y1, edge_y)
    for i in range(ALL):
        c = cond[i]
        if i == MAIN - 1:
            up = c
        elif i == ALL - 1:
            up = turn(cond[MAIN], -32, 1)
        else:
            up = cond[i + 1]
        wx = face(c, up)
        if i == 7:
            wx = wx * open_x0
        if i == 15:
            wx = wx * open_x1
        if i == MAIN + 7:
            wx = wx * jnp.where(block % 2 == 0, open_x0, 1.0)
        if i == MAIN + 3:
            wx = wx * jnp.where(block % 2 == 1, open_x1, 1.0)
        wst[i] = wx
        wy = face(c, turn(c, -1, 1))
        wst[ALL + i] = wy * edge_y if i >= MAIN else wy
        wst[2 * ALL + i] = jnp.where(layer == 7, 0.0, face(c, turn(c, -1, 0)))

    def shape_row(s, i):
        e = est[i]
        p = est[ALL + i] > 0
        scaled = jnp.where(p, e, 100.0) * (ROOT / WIDTH)
        total = jnp.zeros((8, 128), jnp.float32)
        slope = jnp.zeros((8, 128), jnp.float32)
        for j in range(COEF):
            v = scaled - KNOTS[j] * (ROOT / WIDTH)
            b = jnp.exp2(-(v * v))
            bump[(s * COEF + j) * ALL + i] = b
            cb = coef_ref[j] * b
            total = total + cb
            slope = slope + v * cb
        half = jnp.where(p, 1.0, 0.5)
        tst[i] = half * e + total
        sl[s * ALL + i] = half - (2.0 / (WIDTH * ROOT)) * slope

    for s in range(STEPS):
        def one(i, _, s=s):
            shape_row(s, i)
            return 0

        lax.fori_loop(s, MAIN - s, one, 0)
        lax.fori_loop(MAIN, ALL, one, 0)
        state = [est[i] for i in range(ALL)]
        new = advance(
            s, state, lambda i: tst[i], lambda i: wst[i], lambda i: wst[ALL + i], lambda i: wst[2 * ALL + i]
        )
        for i in range(ALL):
            if new[i] is not state[i]:
                est[i] = new[i]

    done = merge([est[i] for i in range(MAIN)], [est[MAIN + g] for g in range(STRIP)])
    for x in range(8):
        e_out[pl.ds(x, 8, stride=8), :] = done[x]

    for dx, dy in corners:
        send_p(1, dx, dy).wait()

    e7 = e_out[56:64, :]
    p7 = el[120:128, :] > 0
    scaled7 = jnp.where(p7, e7, 100.0) * (ROOT / WIDTH)
    slope7 = jnp.zeros((8, 128), jnp.float32)
    for j in range(COEF):
        v = scaled7 - KNOTS[j] * (ROOT / WIDTH)
        b = jnp.exp2(-(v * v))
        v_out[j * 8 : j * 8 + 8, :] = b
        slope7 = slope7 + v * (coef_ref[j] * b)
    slope7 = jnp.where(p7, 1.0, 0.5) - (2.0 / (WIDTH * ROOT)) * slope7

    def pair(q, _):
        for d in range(2):
            send_t(q, d).wait()
        for par in range(2):
            j = q * 2 + par
            main = rows_of(t_ref, hx_t, q * 128 + par * 64)
            state = main + strips_of(main, q + 1, par)
            for s in range(STEPS):
                def temp(i, s=s, state=state):
                    return sl[s * ALL + i] * state[i] + bump[(s * COEF + j) * ALL + i]

                state = advance(
                    s, state, temp, lambda i: wst[i], lambda i: wst[ALL + i], lambda i: wst[2 * ALL + i]
                )
            done = merge(state[:MAIN], state[MAIN:])
            for x in range(8):
                t_out[pl.ds(q * 128 + par * 64 + x, 8, stride=8), :] = done[x]
            at7 = pl.ds(pl.multiple_of(q * 128 + par * 64 + 56, 8), 8)
            to = pl.ds(pl.multiple_of(q * 16 + par * 8, 8), 8)
            v_out[to, :] = slope7 * t_out[at7, :] + v_out[to, :]
        return 0

    lax.fori_loop(0, 8, pair, 0)


def nt(a, b):
    return lax.dot_general(a, b, (((1,), (1,)), ((), ())), preferred_element_type=jnp.float32)


def rows_kernel(
    n_gx, n_gy,
    v_ref, cell_ref, slot_ref, out_ref,
    a_ref, m_ref, snd, rcv, lhs, rhs, local_sem, send_sem, recv_sem,
):
    n = n_gx * n_gy
    gx, gy = lax.axis_index("gx"), lax.axis_index("gy")
    me = gx * n_gy + gy
    barrier = pltpu.get_barrier_semaphore()

    def other(i):
        t = lax.rem(me + i, n)
        return t, (t // n_gy, lax.rem(t, n_gy))

    def greet(i, _):
        pl.semaphore_signal(barrier, inc=1, device_id=other(i)[1], device_id_type=MESH)
        return 0

    lax.fori_loop(1, n, greet, 0)

    bf = jnp.bfloat16
    f32 = jnp.float32
    tall = lax.broadcasted_iota(jnp.int32, (128, 128), 0).astype(f32)
    wide = lax.broadcasted_iota(jnp.int32, (128, 128), 1).astype(f32)
    eight = lax.broadcasted_iota(jnp.int32, (8, 128), 0).astype(f32)

    def hot(rows, row):
        return jnp.where(rows == row, 1.0, 0.0)

    cell, slot = cell_ref[...], slot_ref[...]
    owner = (slot // 1024).astype(f32)
    row = slot % 1024
    row_hi, row_lo = (row // 128 + 1).astype(f32), (row % 128).astype(f32)
    cell_x, cell_y = (cell // 128).astype(f32), (cell % 128).astype(f32)
    by_cell = jnp.zeros((24, 128), f32)
    for b in range(8):
        here = hot(eight, cell_x[b : b + 1])
        left = jnp.concatenate([here * w[b : b + 1] for w in (owner, row_hi, row_lo)], 0)
        by_cell = by_cell + nt(left.astype(bf), hot(tall, cell_y[b : b + 1]).astype(bf))
    owner, row_hi, row_lo = by_cell[0:8], by_cell[8:16], by_cell[16:24]

    before = jnp.where(tall < wide, 1.0, 0.0).astype(bf)
    ones = jnp.ones((128, 128), bf)
    seen = jnp.zeros((128, 128), f32)
    slot_k = lax.broadcasted_iota(jnp.int32, (MOST, 128), 0).astype(f32)
    for x in range(8):
        mine = hot(tall, owner[x : x + 1])
        mine_b = mine.astype(bf)
        a_ref[:, x * 128 : (x + 1) * 128] = mine_b
        count = jnp.dot(mine_b, before, preferred_element_type=f32) + jnp.dot(
            seen.astype(bf), ones, preferred_element_type=f32
        )
        seen = seen + mine
        place = jnp.sum(mine * count, axis=0, keepdims=True)
        at_k = hot(slot_k, place)
        cols = slice(x * 128, (x + 1) * 128)
        for f in range(COEF):
            val = v_ref[f * 8 + x : f * 8 + x + 1, :]
            hi = val.astype(bf).astype(f32)
            lo = val - hi
            m_ref[f * MOST : (f + 1) * MOST, cols] = (at_k * hi).astype(bf)
            m_ref[(COEF + f) * MOST : (COEF + f + 1) * MOST, cols] = (at_k * lo).astype(bf)
        base = 2 * COEF * MOST
        m_ref[base : base + MOST, cols] = (at_k * row_hi[x : x + 1]).astype(bf)
        m_ref[base + MOST : base + 2 * MOST, cols] = (at_k * row_lo[x : x + 1]).astype(bf)
        m_ref[base + 2 * MOST : base + 4 * MOST, cols] = jnp.zeros((2 * MOST, 128), bf)

    for g in range(4):
        hi = nt(a_ref[...], m_ref[g * 128 : (g + 1) * 128, :])
        lo = nt(a_ref[...], m_ref[512 + g * 128 : 512 + (g + 1) * 128, :])
        snd[g] = hi + lo
    snd[4] = nt(a_ref[...], m_ref[1024:1152, :])

    pl.semaphore_wait(barrier, n - 1)
    mine = pl.ds(me, 1)
    own = pltpu.make_async_copy(snd.at[:, mine, :], rcv.at[:, mine, :], local_sem)
    own.start()

    def send(i, _):
        t, device = other(i)
        pltpu.make_async_remote_copy(
            snd.at[:, pl.ds(t, 1), :], rcv.at[:, mine, :], send_sem, recv_sem, device_id=device, device_id_type=MESH
        ).start()
        return 0

    lax.fori_loop(1, n, send, 0)
    own.wait()
    rest = pl.ds(0, n - 1)
    pltpu.make_async_remote_copy(
        snd.at[:, rest, :], rcv.at[:, rest, :], send_sem, recv_sem, device_id=other(1)[1], device_id_type=MESH
    ).wait()

    where = rcv[4].T
    vals = [rcv[g].T for g in range(4)]
    for k in range(MOST):
        cols = slice(k * 128, (k + 1) * 128)
        rhs[:, cols] = hot(tall, where[MOST + k : MOST + k + 1]).astype(bf)
        at_hi = hot(eight + 1.0, where[k : k + 1])
        for f in range(COEF):
            at = (f % 4) * MOST + k
            part = at_hi * vals[f // 4][at : at + 1]
            hi = part.astype(bf)
            lhs[f * 8 : f * 8 + 8, cols] = part
    whole = lhs[...]
    hi = whole.astype(bf)
    lo = (whole - hi.astype(f32)).astype(bf)
    out_ref[...] = nt(hi, rhs[...]) + nt(lo, rhs[...])


def solution(mesh):
    n_gx, n_gy = mesh.shape["gx"], mesh.shape["gy"]
    f32 = jnp.float32
    vmem = pl.BlockSpec(memory_space=pltpu.VMEM)
    smem = pl.BlockSpec(memory_space=pltpu.SMEM)
    dma = pltpu.SemaphoreType.DMA

    def local(enthalpy_start, tangent_start, labels, curve_parameters, pixel_cells, row_slot):
        e = enthalpy_start.reshape(64, 128)
        t = tangent_start.reshape(1024, 128)
        lab = labels.reshape(64, 128)
        e_end, t_end, v = pl.pallas_call(
            functools.partial(steps_kernel, n_gx, n_gy),
            out_shape=[
                jax.ShapeDtypeStruct((64, 128), f32),
                jax.ShapeDtypeStruct((1024, 128), f32),
                jax.ShapeDtypeStruct((128, 128), f32),
            ],
            in_specs=[vmem, vmem, vmem, smem],
            out_specs=[vmem, vmem, vmem],
            scratch_shapes=[
                pltpu.VMEM((128, 128), f32),
                pltpu.VMEM((2, 128, 128), f32),
                pltpu.VMEM((2, 1024, 128), f32),
                pltpu.VMEM((2, 72, 128), f32),
                pltpu.VMEM((3, 2, 72, 128), f32),
                pltpu.VMEM((2 * ALL, 8, 128), f32),
                pltpu.VMEM((ALL, 8, 128), f32),
                pltpu.VMEM((3 * ALL, 8, 128), f32),
                pltpu.VMEM((STEPS * ALL, 8, 128), f32),
                pltpu.VMEM((STEPS * COEF * ALL, 8, 128), f32),
                dma((2,)), dma((2,)), dma((8, 2)), dma((8, 2)), dma((2, 3, 2)), dma((2, 3, 2)),
            ],
            compiler_params=pltpu.CompilerParams(
                collective_id=0, has_side_effects=True, vmem_limit_bytes=48 * 2**20
            ),
            name="steps",
        )(e, t, lab, curve_parameters)
        rows = pl.pallas_call(
            functools.partial(rows_kernel, n_gx, n_gy),
            out_shape=jax.ShapeDtypeStruct((128, 128), f32),
            in_specs=[vmem, vmem, vmem],
            out_specs=vmem,
            scratch_shapes=[
                pltpu.VMEM((128, 1024), jnp.bfloat16),
                pltpu.VMEM((1152, 1024), jnp.bfloat16),
                pltpu.VMEM((5, 128, 128), f32),
                pltpu.VMEM((5, 128, 128), f32),
                pltpu.VMEM((128, 4096), f32),
                pltpu.VMEM((128, 4096), jnp.bfloat16),
                dma, dma, dma,
            ],
            compiler_params=pltpu.CompilerParams(
                collective_id=1, has_side_effects=True, vmem_limit_bytes=48 * 2**20
            ),
            name="rows",
        )(v, pixel_cells.reshape(8, 128), row_slot.reshape(8, 128))
        return (
            e_end.reshape(8, 8, 128),
            t_end.reshape(COEF, 8, 8, 128),
            rows.reshape(COEF, 1024),
        )

    in_specs = (
        P(None, "gx", "gy"),
        P(None, None, "gx", "gy"),
        P(None, "gx", "gy"),
        P(),
        P(("gx", "gy")),
        P(("gx", "gy")),
    )
    out_specs = (P(None, "gx", "gy"), P(None, None, "gx", "gy"), P(None, ("gx", "gy")))
    return jax.shard_map(local, mesh=mesh, in_specs=in_specs, out_specs=out_specs, check_vma=False)
```

```python
import functools
import math

import jax
import jax.numpy as jnp
from jax import lax
from jax.experimental import pallas as pl
from jax.experimental.pallas import tpu as pltpu
from jax.sharding import PartitionSpec as P

COEF = 16
RATE = 0.15
WIDTH = 0.3
ROOT = math.sqrt(math.log2(math.e))
KNOTS = [-2.0 + 0.25 * (j + 0.5) for j in range(COEF)]

DEEP = 4
ROUNDS = 2
MAIN = 16
STRIP = 4
ALL = MAIN + STRIP
ENTH = COEF
MOST = 32
MESH = pl.DeviceIdType.MESH
F32 = jnp.float32
BF16 = jnp.bfloat16


def lanes():
    return lax.broadcasted_iota(jnp.int32, (8, 128), 1)


def turn(v, shift, axis):
    shift = shift % v.shape[axis]
    return v if shift == 0 else pltpu.roll(v, shift, axis)


def place(v, mask, piece):
    return piece if v is None else jnp.where(mask, piece, v)


def own_strips(rows):
    lane = lanes()
    out = []
    for g in range(STRIP):
        v = None
        for c in (1, 2):
            row = rows[4 * (c - 1) + g]
            v = place(v, lane // 16 == c, turn(row, 16 * c + 4, 1))
            v = place(v, lane // 16 == 4 + c, turn(row, 64 + 16 * c - 116, 1))
        out.append(v)
    return out


def pack_edges(strips, it, last, first):
    lane = lanes()
    for g in range(STRIP):
        here = (lane // 32 == g) & (lane % 16 // 4 == it)
        last = place(last, here, turn(strips[g], 32 * g + 4 * it - 88, 1))
        first = place(first, here, turn(strips[g], 32 * g + 4 * it - 20, 1))
    return last, first


def full_strips(own, low, high, before, after, it):
    lane = lanes()
    block, inside = lane // 16, lane % 16
    out = []
    for g in range(STRIP):
        v = own[g]
        v = place(v, block == 0, turn(low[g], 4, 1))
        v = place(v, block == 3, turn(high[g], 52, 1))
        v = place(v, block == 4, turn(low[g], -52, 1))
        v = place(v, block == 7, turn(high[g], -4, 1))
        at = 32 * g + 4 * it
        first, last = inside < 4, inside >= 12
        v = place(v, ((block == 1) | (block == 2)) & first, turn(before[1], 16 - at, 1))
        v = place(v, (block == 0) & first, turn(before[0], -16 - at, 1))
        v = place(v, (block == 3) & first, turn(before[2], 48 - at, 1))
        v = place(v, ((block == 5) | (block == 6)) & last, turn(after[1], 92 - at, 1))
        v = place(v, (block == 4) & last, turn(after[0], 60 - at, 1))
        v = place(v, (block == 7) & last, turn(after[2], 124 - at, 1))
        out.append(v)
    return out


def merge(state):
    lane = lanes()
    out = []
    for x in range(8):
        c, g = 1 + x // 4, x % 4
        v = jnp.where(lane < 4, turn(state[MAIN + g], -(16 * c + 4), 1), state[x + DEEP])
        out.append(jnp.where(lane >= 124, turn(state[MAIN + g], 124 - (72 + 16 * c), 1), v))
    return out


def advance(step, state, temp, wx, wy, wz):
    new = list(state)

    def own(i, t):
        fy = wy(i) * (turn(t, -1, 1) - t)
        fz = wz(i) * (turn(t, -1, 0) - t)
        return (fy - turn(fy, 1, 1)) + (fz - turn(fz, 1, 0))

    lo, hi = step, MAIN - step
    t = temp(lo)
    t_next = temp(lo + 1)
    flux = wx(lo) * (t_next - t)
    for i in range(lo + 1, hi - 1):
        t, t_next = t_next, temp(i + 1)
        below, flux = flux, wx(i) * (t_next - t)
        new[i] = state[i] + ((flux - below) + own(i, t))
    ts = [temp(i) for i in range(MAIN, ALL)]
    fluxes = [wx(MAIN + g) * ((ts[g + 1] if g < STRIP - 1 else turn(ts[0], -16, 1)) - ts[g]) for g in range(STRIP)]
    for g in range(STRIP):
        below = fluxes[g - 1] if g > 0 else turn(fluxes[-1], 16, 1)
        new[MAIN + g] = state[MAIN + g] + ((fluxes[g] - below) + own(MAIN + g, ts[g]))
    return new


def nt(a, b):
    return lax.dot_general(a, b, (((1,), (1,)), ((), ())), preferred_element_type=F32)


def hot(rows, row):
    return jnp.where(rows == row, 1.0, 0.0)


def kernel(
    n_gx, n_gy,
    e_ref, t_ref, lab_ref, coef_ref, cell_ref, slot_ref,
    e_out, t_out, rows_out,
    e_in, lab_in, own, mid, hx0, hx1, pk, hp, own_st, est, tst, wst, sl, bump,
    a_ref, atk, tab, m_ref, snd, rcv, lhs, rhs,
    in_sem, out_sem, x_send, x_recv, p_send, p_recv, line_sem, local_sem, all_send, all_recv,
):
    n = n_gx * n_gy
    gx, gy = lax.axis_index("gx"), lax.axis_index("gy")
    me = gx * n_gy + gy

    def at(dx, dy):
        return lax.rem(gx + dx + n_gx, n_gx), lax.rem(gy + dy + n_gy, n_gy)

    corners = [(dx, dy) for dx in (0, -1, 1) for dy in (-1, 1)]
    line = [(dx, 0) for dx in range(1, n_gx)]
    greeted = line + [(0, dy) for dy in range(1, n_gy)] + [c for c in corners if c[0] != 0]
    barrier = pltpu.get_barrier_semaphore()
    for dx, dy in greeted:
        pl.semaphore_signal(barrier, inc=1, device_id=at(dx, dy), device_id_type=MESH)

    def load_e():
        return pltpu.make_async_copy(e_ref, e_in, in_sem.at[8])

    def load_lab():
        return pltpu.make_async_copy(lab_ref, lab_in, in_sem.at[9])

    def load_t(x):
        return pltpu.make_async_copy(t_ref.at[:, x, :], own.at[x, pl.ds(0, 128), :], in_sem.at[x])

    load_e().start()
    load_lab().start()
    for x in range(8):
        load_t(x).start()
    load_e().wait()
    load_lab().wait()
    pair = [[], []]
    for x in range(8):
        pair[0].append(e_in[pl.ds(x, 8, stride=8), :])
        pair[1].append(jnp.where(lab_in[pl.ds(x, 8, stride=8), :] == 1, 1.0, 0.0))
        for k in range(2):
            own[x, (ENTH + k) * 8 : (ENTH + k + 1) * 8, :] = pair[k][x]

    halos = (hx0, hx1)

    def send_x(r, q, d):
        part = pl.ds(q * 32, 32) if not isinstance(q, int) or q < 4 else pl.ds(128, 16 if r == 0 else 8)
        source = own if r == 0 else mid
        return pltpu.make_async_remote_copy(
            source.at[pl.ds(DEEP - DEEP * d, DEEP), part, :], halos[r].at[d, :, part, :],
            x_send.at[r, q, d], x_recv.at[r, q, d], device_id=at(1 - 2 * d, 0), device_id_type=MESH,
        )

    def send_p(r, group, dx, dy):
        part = pl.ds(group * 16, 16) if group < 2 else pl.ds(32, 8)
        side = 0 if dy == 1 else 1
        return pltpu.make_async_remote_copy(
            pk.at[r, side, part], hp.at[r, 1 - dx, side, part],
            p_send.at[r, group, dx + 1, side], p_recv.at[r, group, 1 - dx, side],
            device_id=at(dx, dy), device_id_type=MESH,
        )

    def store_pack(r, q, last, first):
        to = pl.ds(pl.multiple_of(q * 8, 8), 8)
        pk[r, 0, to, :] = last
        pk[r, 1, to, :] = first

    def store_strips(item, strips):
        for g in range(STRIP):
            own_st[item * STRIP + g] = strips[g]

    last = first = None
    for k in range(2):
        strips = own_strips(pair[k])
        store_strips(ENTH + k, strips)
        last, first = pack_edges(strips, k, last, first)
    store_pack(0, 4, last, first)

    pl.semaphore_wait(barrier, len(greeted))
    for d in range(2):
        send_x(0, 4, d).start()
    for dx, dy in corners:
        send_p(0, 2, dx, dy).start()
    for dx, dy in line:
        pl.semaphore_signal(line_sem, inc=1, device_id=at(dx, dy), device_id_type=MESH)
    for x in range(8):
        load_t(x).wait()
    for q in range(4):
        for d in range(2):
            send_x(0, q, d).start()

    def own_rows(ref, item):
        part = pl.ds(pl.multiple_of(item * 8, 8), 8)
        return [ref[x, part, :] for x in range(8)]

    def pack_quad(q, _):
        last = first = None
        for it in range(4):
            strips = own_strips(own_rows(own, q * 4 + it))
            store_strips(q * 4 + it, strips)
            last, first = pack_edges(strips, it, last, first)
        store_pack(0, q, last, first)
        return 0

    lax.fori_loop(0, 4, pack_quad, 0)
    for group in range(2):
        for dx, dy in corners:
            send_p(0, group, dx, dy).start()

    tall = lax.broadcasted_iota(jnp.int32, (128, 128), 0).astype(F32)
    wide = lax.broadcasted_iota(jnp.int32, (128, 128), 1).astype(F32)
    eight = lax.broadcasted_iota(jnp.int32, (8, 128), 0).astype(F32)
    cell, slot = cell_ref[...], slot_ref[...]
    owner = (slot // 1024).astype(F32)
    row = slot % 1024
    row_hi, row_lo = (row // 128 + 1).astype(F32), (row % 128).astype(F32)
    cell_x, cell_y = (cell // 128).astype(F32), (cell % 128).astype(F32)
    by_cell = jnp.zeros((24, 128), F32)
    for b in range(8):
        here = hot(eight, cell_x[b : b + 1])
        left = jnp.concatenate([here * w[b : b + 1] for w in (owner, row_hi, row_lo)], 0)
        by_cell = by_cell + nt(left.astype(BF16), hot(tall, cell_y[b : b + 1]).astype(BF16))
    owner, row_hi, row_lo = by_cell[0:8], by_cell[8:16], by_cell[16:24]
    earlier = jnp.where(tall < wide, 1.0, 0.0).astype(BF16)
    ones = jnp.ones((128, 128), BF16)
    seen = jnp.zeros((128, 128), F32)
    slot_k = lax.broadcasted_iota(jnp.int32, (MOST, 128), 0).astype(F32)
    for x in range(8):
        cols = slice(x * 128, (x + 1) * 128)
        mine = hot(tall, owner[x : x + 1])
        mine_b = mine.astype(BF16)
        a_ref[:, cols] = mine_b
        count = jnp.dot(mine_b, earlier, preferred_element_type=F32) + jnp.dot(
            seen.astype(BF16), ones, preferred_element_type=F32
        )
        seen = seen + mine
        at_k = hot(slot_k, jnp.sum(mine * count, axis=0, keepdims=True))
        atk[x] = at_k
        tab[0:MOST, cols] = (at_k * row_hi[x : x + 1]).astype(BF16)
        tab[MOST : 2 * MOST, cols] = (at_k * row_lo[x : x + 1]).astype(BF16)
        tab[2 * MOST : 4 * MOST, cols] = jnp.zeros((2 * MOST, 128), BF16)
    snd[4] = nt(a_ref[...], tab[...])

    def halo_rows(r, d, item):
        part = pl.ds(pl.multiple_of(item * 8, 8), 8)
        return [halos[r][d, x, part, :] for x in range(DEEP)]

    def all_rows(r, item, q, it):
        low, high = halo_rows(r, 0, item), halo_rows(r, 1, item)
        main = low + own_rows(own if r == 0 else mid, item) + high
        part = pl.ds(pl.multiple_of(q * 8, 8), 8)
        before = [hp[r, k, 0, part, :] for k in range(3)]
        after = [hp[r, k, 1, part, :] for k in range(3)]
        strips = [own_st[item * STRIP + g] for g in range(STRIP)]
        return main + full_strips(strips, low, high, before, after, it)

    def wait_e(r):
        for d in range(2):
            send_x(r, 4, d).wait()
        for dx, dy in corners:
            send_p(r, 2, dx, dy).wait()

    wait_e(0)
    pcm = all_rows(0, ENTH + 1, 4, 1)
    for i in range(ALL):
        est[ALL + i] = pcm[i]

    lane = lanes()
    block, inside = lane // 16, lane % 16
    layer = lax.broadcasted_iota(jnp.int32, (8, 128), 0)
    open_x0 = jnp.where(gx == 0, 0.0, 1.0)
    open_x1 = jnp.where(gx == n_gx - 1, 0.0, 1.0)
    open_y0 = jnp.where(gy == 0, 0.0, 1.0)
    open_y1 = jnp.where(gy == n_gy - 1, 0.0, 1.0)
    cond = [1.0 - 0.5 * p for p in pcm]

    def face(a, b):
        return (2.0 * RATE) * a * b / (a + b)

    edge_y = jnp.where((block < 4) & (inside == 3), open_y0, 1.0)
    edge_y = jnp.where((block >= 4) & (inside == 11), open_y1, edge_y)
    edge_x = jnp.where((block == 0) | (block == 4), open_x0, 1.0)
    edge_x = jnp.where((block == 2) | (block == 6), open_x1, edge_x)
    for i in range(ALL):
        c = cond[i]
        if i == MAIN - 1:
            up = c
        elif i == ALL - 1:
            up = turn(cond[MAIN], -16, 1)
        else:
            up = cond[i + 1]
        wx = face(c, up)
        if i == 3:
            wx = wx * open_x0
        if i == 11:
            wx = wx * open_x1
        if i == ALL - 1:
            wx = wx * edge_x
        wst[i] = wx
        wy = face(c, turn(c, -1, 1))
        wst[ALL + i] = wy * edge_y if i >= MAIN else wy
        wst[2 * ALL + i] = jnp.where(layer == 7, 0.0, face(c, turn(c, -1, 0)))

    weights = (lambda i: wst[i], lambda i: wst[ALL + i], lambda i: wst[2 * ALL + i])

    def shape_row(s, i):
        e = est[i]
        p = est[ALL + i] > 0
        scaled = jnp.where(p, e, 100.0) * (ROOT / WIDTH)
        total = jnp.zeros((8, 128), F32)
        slope = jnp.zeros((8, 128), F32)
        for j in range(COEF):
            v = scaled - KNOTS[j] * (ROOT / WIDTH)
            b = jnp.exp2(-(v * v))
            bump[(s * COEF + j) * ALL + i] = b
            cb = coef_ref[j] * b
            total = total + cb
            slope = slope + v * cb
        half = jnp.where(p, 1.0, 0.5)
        tst[i] = half * e + total
        sl[s * ALL + i] = half - (2.0 / (WIDTH * ROOT)) * slope

    def shape_rows(s, lo, hi):
        for i in range(lo, lo + (hi - lo) % 4):
            shape_row(s, i)
        lo += (hi - lo) % 4

        def four(k, _):
            for i in range(4):
                shape_row(s, lo + k * 4 + i)
            return 0

        lax.fori_loop(0, (hi - lo) // 4, four, 0)

    def enthalpy(r):
        start = all_rows(r, ENTH, 4, 0)
        for i in range(ALL):
            est[i] = start[i]
        for s in range(DEEP):
            shape_rows(s, s, MAIN - s)
            shape_rows(s, MAIN, ALL)
            state = [est[i] for i in range(ALL)]
            new = advance(s, state, lambda i: tst[i], *weights)
            for i in range(ALL):
                if new[i] is not state[i]:
                    est[i] = new[i]
        state = [est[i] for i in range(ALL)]
        done = merge(state)
        for x in range(8):
            mid[x, ENTH * 8 : ENTH * 8 + 8, :] = done[x]
        if r == 0:
            store_strips(ENTH, state[MAIN:])
            last, first = pack_edges(state[MAIN:], 0, None, None)
            store_pack(1, 4, last, first)

    def tangents(r, q):
        last = first = None
        for it in range(4):
            j = q * 4 + it
            state = all_rows(r, j, q, it)
            for s in range(DEEP):
                def temp(i, s=s, state=state):
                    return sl[s * ALL + i] * state[i] + bump[(s * COEF + j) * ALL + i]

                state = advance(s, state, temp, *weights)
            done = merge(state)
            part = pl.ds(pl.multiple_of(j * 8, 8), 8)
            for x in range(8):
                mid[x, part, :] = done[x]
            if r == 0:
                store_strips(j, state[MAIN:])
                last, first = pack_edges(state[MAIN:], it, last, first)
        if r == 0:
            store_pack(1, q, last, first)

    enthalpy(0)
    for d in range(2):
        send_x(1, 4, d).start()
    for dx, dy in corners:
        send_p(1, 2, dx, dy).start()
    for group in range(2):
        for dx, dy in corners:
            send_p(0, group, dx, dy).wait()

    def first_round(q, _):
        for d in range(2):
            send_x(0, q, d).wait()
        tangents(0, q)
        for d in range(2):
            send_x(1, q, d).start()
        for group in range(2):
            @pl.when(q == 2 * group + 1)
            def _():
                for dx, dy in corners:
                    send_p(1, group, dx, dy).start()
        return 0

    lax.fori_loop(0, 4, first_round, 0)
    wait_e(1)
    enthalpy(1)

    def second_round(q, _):
        for group in range(2):
            @pl.when(q == 2 * group)
            def _():
                for dx, dy in corners:
                    send_p(1, group, dx, dy).wait()
        for d in range(2):
            send_x(1, q, d).wait()
        tangents(1, q)
        return 0

    lax.fori_loop(0, 4, second_round, 0)

    def store_t(x):
        return pltpu.make_async_copy(mid.at[x, pl.ds(0, 128), :], t_out.at[:, x, :], out_sem.at[x])

    def store_e():
        return pltpu.make_async_copy(e_in, e_out, out_sem.at[8])

    for x in range(8):
        e_in[pl.ds(x, 8, stride=8), :] = mid[x, ENTH * 8 : ENTH * 8 + 8, :]
    store_e().start()
    for x in range(8):
        store_t(x).start()

    def top(item):
        v = jnp.broadcast_to(mid[0, item * 8 + 7 : item * 8 + 8, :], (8, 128))
        for x in range(1, 8):
            v = jnp.where(eight == x, mid[x, item * 8 + 7 : item * 8 + 8, :], v)
        return v

    p7 = jnp.where(lab_in[56:64, :] == 1, 1.0, 0.0) > 0
    scaled = jnp.where(p7, top(ENTH), 100.0) * (ROOT / WIDTH)
    slope = jnp.zeros((8, 128), F32)
    bumps = []
    for j in range(COEF):
        v = scaled - KNOTS[j] * (ROOT / WIDTH)
        b = jnp.exp2(-(v * v))
        bumps.append(b)
        slope = slope + v * (coef_ref[j] * b)
    slope = jnp.where(p7, 1.0, 0.5) - (2.0 / (WIDTH * ROOT)) * slope
    for f in range(COEF):
        val = slope * top(f) + bumps[f]
        hi = val.astype(BF16).astype(F32)
        lo = val - hi
        for x in range(8):
            cols = slice(x * 128, (x + 1) * 128)
            at_k = atk[x]
            m_ref[f * MOST : (f + 1) * MOST, cols] = (at_k * hi[x : x + 1]).astype(BF16)
            m_ref[(COEF + f) * MOST : (COEF + f + 1) * MOST, cols] = (at_k * lo[x : x + 1]).astype(BF16)
    for g in range(4):
        hi = nt(a_ref[...], m_ref[g * 128 : (g + 1) * 128, :])
        lo = nt(a_ref[...], m_ref[512 + g * 128 : 512 + (g + 1) * 128, :])
        snd[g] = hi + lo

    pl.semaphore_wait(line_sem, len(line))
    mine = pl.ds(me, 1)
    keep = pltpu.make_async_copy(snd.at[:, mine, :], rcv.at[:, mine, :], local_sem)
    keep.start()

    def send_rows(i, _):
        t = lax.rem(me + i, n)
        pltpu.make_async_remote_copy(
            snd.at[:, pl.ds(t, 1), :], rcv.at[:, mine, :], all_send, all_recv,
            device_id=(t // n_gy, lax.rem(t, n_gy)), device_id_type=MESH,
        ).start()
        return 0

    lax.fori_loop(1, n, send_rows, 0)
    keep.wait()
    rest = pl.ds(0, n - 1)
    pltpu.make_async_remote_copy(
        snd.at[:, rest, :], rcv.at[:, rest, :], all_send, all_recv, device_id=at(1, 0), device_id_type=MESH
    ).wait()

    where = rcv[4].T
    vals = [rcv[g].T for g in range(4)]
    for k in range(MOST):
        cols = slice(k * 128, (k + 1) * 128)
        rhs[:, cols] = hot(tall, where[MOST + k : MOST + k + 1]).astype(BF16)
        at_hi = hot(eight + 1.0, where[k : k + 1])
        for f in range(COEF):
            at_f = (f % 4) * MOST + k
            lhs[f * 8 : f * 8 + 8, cols] = at_hi * vals[f // 4][at_f : at_f + 1]
    whole = lhs[...]
    hi = whole.astype(BF16)
    lo = (whole - hi.astype(F32)).astype(BF16)
    rows_out[...] = nt(hi, rhs[...]) + nt(lo, rhs[...])
    store_e().wait()
    for x in range(8):
        store_t(x).wait()


def solution(mesh):
    n_gx, n_gy = mesh.shape["gx"], mesh.shape["gy"]
    vmem = pl.BlockSpec(memory_space=pltpu.VMEM)
    smem = pl.BlockSpec(memory_space=pltpu.SMEM)
    hbm = pl.BlockSpec(memory_space=pl.ANY)
    dma = pltpu.SemaphoreType.DMA

    def tiles(*shape):
        return pltpu.VMEM((*shape, 8, 128), F32)

    def local(enthalpy_start, tangent_start, labels, curve_parameters, pixel_cells, row_slot):
        e_end, t_end, rows = pl.pallas_call(
            functools.partial(kernel, n_gx, n_gy),
            out_shape=[
                jax.ShapeDtypeStruct((64, 128), F32),
                jax.ShapeDtypeStruct((128, 8, 128), F32),
                jax.ShapeDtypeStruct((128, 128), F32),
            ],
            in_specs=[hbm, hbm, hbm, smem, vmem, vmem],
            out_specs=[hbm, hbm, vmem],
            scratch_shapes=[
                pltpu.VMEM((64, 128), F32),
                pltpu.VMEM((64, 128), jnp.int32),
                pltpu.VMEM((8, 144, 128), F32),
                pltpu.VMEM((8, 136, 128), F32),
                pltpu.VMEM((2, DEEP, 144, 128), F32),
                pltpu.VMEM((2, DEEP, 136, 128), F32),
                pltpu.VMEM((ROUNDS, 2, 40, 128), F32),
                pltpu.VMEM((ROUNDS, 3, 2, 40, 128), F32),
                tiles((COEF + 2) * STRIP),
                tiles(2 * ALL),
                tiles(ALL),
                tiles(3 * ALL),
                tiles(DEEP * ALL),
                tiles(DEEP * COEF * ALL),
                pltpu.VMEM((128, 1024), BF16),
                pltpu.VMEM((8, MOST, 128), F32),
                pltpu.VMEM((128, 1024), BF16),
                pltpu.VMEM((1024, 1024), BF16),
                pltpu.VMEM((5, 128, 128), F32),
                pltpu.VMEM((5, 128, 128), F32),
                pltpu.VMEM((128, 4096), F32),
                pltpu.VMEM((128, 4096), BF16),
                dma((10,)), dma((9,)),
                dma((ROUNDS, 5, 2)), dma((ROUNDS, 5, 2)),
                dma((ROUNDS, 3, 3, 2)), dma((ROUNDS, 3, 3, 2)),
                pltpu.SemaphoreType.REGULAR, dma, dma, dma,
            ],
            compiler_params=pltpu.CompilerParams(
                collective_id=0, has_side_effects=True, vmem_limit_bytes=48 * 2**20
            ),
            name="steps",
        )(
            enthalpy_start.reshape(64, 128), tangent_start.reshape(128, 8, 128), labels.reshape(64, 128),
            curve_parameters, pixel_cells.reshape(8, 128), row_slot.reshape(8, 128),
        )
        return (
            e_end.reshape(8, 8, 128),
            t_end.reshape(COEF, 8, 8, 128),
            rows.reshape(COEF, 1024),
        )

    in_specs = (
        P(None, "gx", "gy"),
        P(None, None, "gx", "gy"),
        P(None, "gx", "gy"),
        P(),
        P(("gx", "gy")),
        P(("gx", "gy")),
    )
    out_specs = (P(None, "gx", "gy"), P(None, None, "gx", "gy"), P(None, ("gx", "gy")))
    return jax.shard_map(local, mesh=mesh, in_specs=in_specs, out_specs=out_specs, check_vma=False)
```

```python
import functools
import math

import jax
import jax.numpy as jnp
from jax import lax
from jax.experimental import pallas as pl
from jax.experimental.pallas import tpu as pltpu
from jax.sharding import PartitionSpec as P

COEF = 16
RATE = 0.15
WIDTH = 0.3
ROOT = math.sqrt(math.log2(math.e))
KNOTS = [-2.0 + 0.25 * (j + 0.5) for j in range(COEF)]

DEEP = 4
ROUNDS = 2
MAIN = 16
STRIP = 4
ALL = MAIN + STRIP
ENTH = COEF
MOST = 32
MESH = pl.DeviceIdType.MESH
F32 = jnp.float32
BF16 = jnp.bfloat16


def lanes():
    return lax.broadcasted_iota(jnp.int32, (8, 128), 1)


def turn(v, shift, axis):
    shift = shift % v.shape[axis]
    return v if shift == 0 else pltpu.roll(v, shift, axis)


def place(v, mask, piece):
    return piece if v is None else jnp.where(mask, piece, v)


def own_strips(rows):
    lane = lanes()
    out = []
    for g in range(STRIP):
        v = None
        for c in (1, 2):
            row = rows[4 * (c - 1) + g]
            v = place(v, lane // 16 == c, turn(row, 16 * c + 4, 1))
            v = place(v, lane // 16 == 4 + c, turn(row, 64 + 16 * c - 116, 1))
        out.append(v)
    return out


def pack_edges(strips, it, last, first):
    lane = lanes()
    for g in range(STRIP):
        here = (lane // 32 == g) & (lane % 16 // 4 == it)
        last = place(last, here, turn(strips[g], 32 * g + 4 * it - 88, 1))
        first = place(first, here, turn(strips[g], 32 * g + 4 * it - 20, 1))
    return last, first


def full_strips(own, low, high, before, after, it):
    lane = lanes()
    block, inside = lane // 16, lane % 16
    out = []
    for g in range(STRIP):
        v = own[g]
        v = place(v, block == 0, turn(low[g], 4, 1))
        v = place(v, block == 3, turn(high[g], 52, 1))
        v = place(v, block == 4, turn(low[g], -52, 1))
        v = place(v, block == 7, turn(high[g], -4, 1))
        at = 32 * g + 4 * it
        first, last = inside < 4, inside >= 12
        v = place(v, ((block == 1) | (block == 2)) & first, turn(before[1], 16 - at, 1))
        v = place(v, (block == 0) & first, turn(before[0], -16 - at, 1))
        v = place(v, (block == 3) & first, turn(before[2], 48 - at, 1))
        v = place(v, ((block == 5) | (block == 6)) & last, turn(after[1], 92 - at, 1))
        v = place(v, (block == 4) & last, turn(after[0], 60 - at, 1))
        v = place(v, (block == 7) & last, turn(after[2], 124 - at, 1))
        out.append(v)
    return out


def merge(state):
    lane = lanes()
    out = []
    for x in range(8):
        c, g = 1 + x // 4, x % 4
        v = jnp.where(lane < 4, turn(state[MAIN + g], -(16 * c + 4), 1), state[x + DEEP])
        out.append(jnp.where(lane >= 124, turn(state[MAIN + g], 124 - (72 + 16 * c), 1), v))
    return out


def advance(step, state, temp, wx, wy, wz):
    new = list(state)

    def own(i, t):
        fy = wy(i) * (turn(t, -1, 1) - t)
        fz = wz(i) * (turn(t, -1, 0) - t)
        return (fy - turn(fy, 1, 1)) + (fz - turn(fz, 1, 0))

    lo, hi = step, MAIN - step
    t = temp(lo)
    t_next = temp(lo + 1)
    flux = wx(lo) * (t_next - t)
    for i in range(lo + 1, hi - 1):
        t, t_next = t_next, temp(i + 1)
        below, flux = flux, wx(i) * (t_next - t)
        new[i] = state[i] + ((flux - below) + own(i, t))
    ts = [temp(i) for i in range(MAIN, ALL)]
    fluxes = [wx(MAIN + g) * ((ts[g + 1] if g < STRIP - 1 else turn(ts[0], -16, 1)) - ts[g]) for g in range(STRIP)]
    for g in range(STRIP):
        below = fluxes[g - 1] if g > 0 else turn(fluxes[-1], 16, 1)
        new[MAIN + g] = state[MAIN + g] + ((fluxes[g] - below) + own(MAIN + g, ts[g]))
    return new


def nt(a, b):
    return lax.dot_general(a, b, (((1,), (1,)), ((), ())), preferred_element_type=F32)


def hot(rows, row):
    return jnp.where(rows == row, 1.0, 0.0)


def kernel(
    n_gx, n_gy,
    e_ref, t_ref, lab_ref, coef_ref, cell_ref, slot_ref,
    mid, rcv,
    e_in, lab_in, cell_in, slot_in, coef_in, own, hx0, hx1, pk, hp, own_st, est, tst, wst, sl, bump,
    a_ref, atk, tab, m_ref, snd,
    in_sem, x_send, x_recv, p_send, p_recv, line_sem, local_sem, all_send, all_recv,
):
    n = n_gx * n_gy
    gx, gy = lax.axis_index("gx"), lax.axis_index("gy")
    me = gx * n_gy + gy

    def at(dx, dy):
        return lax.rem(gx + dx + n_gx, n_gx), lax.rem(gy + dy + n_gy, n_gy)

    corners = [(dx, dy) for dx in (0, -1, 1) for dy in (-1, 1)]
    line = [(dx, 0) for dx in range(1, n_gx)]
    greeted = line + [(0, dy) for dy in range(1, n_gy)] + [c for c in corners if c[0] != 0]
    barrier = pltpu.get_barrier_semaphore()
    for dx, dy in greeted:
        pl.semaphore_signal(barrier, inc=1, device_id=at(dx, dy), device_id_type=MESH)

    def load_e():
        return pltpu.make_async_copy(e_ref, e_in, in_sem.at[8])

    def load_lab():
        return pltpu.make_async_copy(lab_ref, lab_in, in_sem.at[9])

    def load_t(x):
        return pltpu.make_async_copy(t_ref.at[:, x, :], own.at[x, pl.ds(0, 128), :], in_sem.at[x])

    def load_cell():
        return pltpu.make_async_copy(cell_ref, cell_in, in_sem.at[10])

    def load_slot():
        return pltpu.make_async_copy(slot_ref, slot_in, in_sem.at[11])

    def load_coef():
        return pltpu.make_async_copy(coef_ref, coef_in, in_sem.at[12])

    load_e().start()
    load_lab().start()
    for x in range(8):
        load_t(x).start()
    load_cell().start()
    load_slot().start()
    load_coef().start()
    load_e().wait()
    load_lab().wait()
    pair = [[], []]
    for x in range(8):
        pair[0].append(e_in[pl.ds(x, 8, stride=8), :])
        pair[1].append(jnp.where(lab_in[pl.ds(x, 8, stride=8), :] == 1, 1.0, 0.0))
        for k in range(2):
            own[x, (ENTH + k) * 8 : (ENTH + k + 1) * 8, :] = pair[k][x]

    halos = (hx0, hx1)

    def send_x(r, q, d):
        part = pl.ds(q * 32, 32) if not isinstance(q, int) or q < 4 else pl.ds(128, 16 if r == 0 else 8)
        source = own if r == 0 else mid
        return pltpu.make_async_remote_copy(
            source.at[pl.ds(DEEP - DEEP * d, DEEP), part, :], halos[r].at[d, :, part, :],
            x_send.at[r, q, d], x_recv.at[r, q, d], device_id=at(1 - 2 * d, 0), device_id_type=MESH,
        )

    def send_p(r, group, dx, dy):
        part = pl.ds(group * 16, 16) if group < 2 else pl.ds(32, 8)
        side = 0 if dy == 1 else 1
        return pltpu.make_async_remote_copy(
            pk.at[r, side, part], hp.at[r, 1 - dx, side, part],
            p_send.at[r, group, dx + 1, side], p_recv.at[r, group, 1 - dx, side],
            device_id=at(dx, dy), device_id_type=MESH,
        )

    def store_pack(r, q, last, first):
        to = pl.ds(pl.multiple_of(q * 8, 8), 8)
        pk[r, 0, to, :] = last
        pk[r, 1, to, :] = first

    def store_strips(item, strips):
        for g in range(STRIP):
            own_st[item * STRIP + g] = strips[g]

    last = first = None
    for k in range(2):
        strips = own_strips(pair[k])
        store_strips(ENTH + k, strips)
        last, first = pack_edges(strips, k, last, first)
    store_pack(0, 4, last, first)

    pl.semaphore_wait(barrier, len(greeted))
    for d in range(2):
        send_x(0, 4, d).start()
    for dx, dy in corners:
        send_p(0, 2, dx, dy).start()
    for dx, dy in line:
        pl.semaphore_signal(line_sem, inc=1, device_id=at(dx, dy), device_id_type=MESH)
    for x in range(8):
        load_t(x).wait()
    for d in range(2):
        send_x(0, 0, d).start()

    def own_rows(ref, item):
        part = pl.ds(pl.multiple_of(item * 8, 8), 8)
        return [ref[x, part, :] for x in range(8)]

    def pack_quad(q, _):
        last = first = None
        for it in range(4):
            strips = own_strips(own_rows(own, q * 4 + it))
            store_strips(q * 4 + it, strips)
            last, first = pack_edges(strips, it, last, first)
        store_pack(0, q, last, first)
        return 0

    lax.fori_loop(0, 4, pack_quad, 0)
    for group in range(2):
        for dx, dy in corners:
            send_p(0, group, dx, dy).start()
    for q in range(1, 4):
        for d in range(2):
            send_x(0, q, d).start()

    tall = lax.broadcasted_iota(jnp.int32, (128, 128), 0).astype(F32)
    wide = lax.broadcasted_iota(jnp.int32, (128, 128), 1).astype(F32)
    eight = lax.broadcasted_iota(jnp.int32, (8, 128), 0).astype(F32)
    load_cell().wait()
    load_slot().wait()
    load_coef().wait()
    cell, slot = cell_in[...], slot_in[...]
    owner = (slot // 1024).astype(F32)
    row = slot % 1024
    row_hi, row_lo = (row // 128 + 1).astype(F32), (row % 128).astype(F32)
    cell_x, cell_y = (cell // 128).astype(F32), (cell % 128).astype(F32)
    by_cell = jnp.zeros((24, 128), F32)
    for b in range(8):
        here = hot(eight, cell_x[b : b + 1])
        left = jnp.concatenate([here * w[b : b + 1] for w in (owner, row_hi, row_lo)], 0)
        by_cell = by_cell + nt(left.astype(BF16), hot(tall, cell_y[b : b + 1]).astype(BF16))
    owner, row_hi, row_lo = by_cell[0:8], by_cell[8:16], by_cell[16:24]
    earlier = jnp.where(tall < wide, 1.0, 0.0).astype(BF16)
    ones = jnp.ones((128, 128), BF16)
    seen = jnp.zeros((128, 128), F32)
    slot_k = lax.broadcasted_iota(jnp.int32, (MOST, 128), 0).astype(F32)
    for x in range(8):
        cols = slice(x * 128, (x + 1) * 128)
        mine = hot(tall, owner[x : x + 1])
        mine_b = mine.astype(BF16)
        a_ref[:, cols] = mine_b
        count = jnp.dot(mine_b, earlier, preferred_element_type=F32) + jnp.dot(
            seen.astype(BF16), ones, preferred_element_type=F32
        )
        seen = seen + mine
        at_k = hot(slot_k, jnp.sum(mine * count, axis=0, keepdims=True))
        atk[x] = at_k
        tab[0:MOST, cols] = (at_k * row_hi[x : x + 1]).astype(BF16)
        tab[MOST : 2 * MOST, cols] = (at_k * row_lo[x : x + 1]).astype(BF16)
        tab[2 * MOST : 4 * MOST, cols] = jnp.zeros((2 * MOST, 128), BF16)
    snd[4] = nt(a_ref[...], tab[...])

    def halo_rows(r, d, item):
        part = pl.ds(pl.multiple_of(item * 8, 8), 8)
        return [halos[r][d, x, part, :] for x in range(DEEP)]

    def all_rows(r, item, q, it):
        low, high = halo_rows(r, 0, item), halo_rows(r, 1, item)
        main = low + own_rows(own if r == 0 else mid, item) + high
        part = pl.ds(pl.multiple_of(q * 8, 8), 8)
        before = [hp[r, k, 0, part, :] for k in range(3)]
        after = [hp[r, k, 1, part, :] for k in range(3)]
        strips = [own_st[item * STRIP + g] for g in range(STRIP)]
        return main + full_strips(strips, low, high, before, after, it)

    def wait_e(r):
        for d in range(2):
            send_x(r, 4, d).wait()
        for dx, dy in corners:
            send_p(r, 2, dx, dy).wait()

    wait_e(0)
    pcm = all_rows(0, ENTH + 1, 4, 1)
    for i in range(ALL):
        est[ALL + i] = pcm[i]

    lane = lanes()
    block, inside = lane // 16, lane % 16
    layer = lax.broadcasted_iota(jnp.int32, (8, 128), 0)
    open_x0 = jnp.where(gx == 0, 0.0, 1.0)
    open_x1 = jnp.where(gx == n_gx - 1, 0.0, 1.0)
    open_y0 = jnp.where(gy == 0, 0.0, 1.0)
    open_y1 = jnp.where(gy == n_gy - 1, 0.0, 1.0)
    cond = [1.0 - 0.5 * p for p in pcm]

    def face(a, b):
        return (2.0 * RATE) * a * b / (a + b)

    edge_y = jnp.where((block < 4) & (inside == 3), open_y0, 1.0)
    edge_y = jnp.where((block >= 4) & (inside == 11), open_y1, edge_y)
    edge_x = jnp.where((block == 0) | (block == 4), open_x0, 1.0)
    edge_x = jnp.where((block == 2) | (block == 6), open_x1, edge_x)
    for i in range(ALL):
        c = cond[i]
        if i == MAIN - 1:
            up = c
        elif i == ALL - 1:
            up = turn(cond[MAIN], -16, 1)
        else:
            up = cond[i + 1]
        wx = face(c, up)
        if i == 3:
            wx = wx * open_x0
        if i == 11:
            wx = wx * open_x1
        if i == ALL - 1:
            wx = wx * edge_x
        wst[i] = wx
        wy = face(c, turn(c, -1, 1))
        wst[ALL + i] = wy * edge_y if i >= MAIN else wy
        wst[2 * ALL + i] = jnp.where(layer == 7, 0.0, face(c, turn(c, -1, 0)))

    weights = (lambda i: wst[i], lambda i: wst[ALL + i], lambda i: wst[2 * ALL + i])

    def shape_row(s, i):
        e = est[i]
        p = est[ALL + i] > 0
        scaled = jnp.where(p, e, 100.0) * (ROOT / WIDTH)
        total = jnp.zeros((8, 128), F32)
        slope = jnp.zeros((8, 128), F32)
        for j in range(COEF):
            v = scaled - KNOTS[j] * (ROOT / WIDTH)
            b = jnp.exp2(-(v * v))
            bump[(s * COEF + j) * ALL + i] = b
            cb = coef_in[j] * b
            total = total + cb
            slope = slope + v * cb
        half = jnp.where(p, 1.0, 0.5)
        tst[i] = half * e + total
        sl[s * ALL + i] = half - (2.0 / (WIDTH * ROOT)) * slope

    def shape_rows(s, lo, hi):
        for i in range(lo, lo + (hi - lo) % 4):
            shape_row(s, i)
        lo += (hi - lo) % 4

        def four(k, _):
            for i in range(4):
                shape_row(s, lo + k * 4 + i)
            return 0

        lax.fori_loop(0, (hi - lo) // 4, four, 0)

    def enthalpy(r):
        start = all_rows(r, ENTH, 4, 0)
        for i in range(ALL):
            est[i] = start[i]
        for s in range(DEEP):
            shape_rows(s, s, MAIN - s)
            shape_rows(s, MAIN, ALL)
            state = [est[i] for i in range(ALL)]
            new = advance(s, state, lambda i: tst[i], *weights)
            for i in range(ALL):
                if new[i] is not state[i]:
                    est[i] = new[i]
        state = [est[i] for i in range(ALL)]
        done = merge(state)
        for x in range(8):
            mid[x, ENTH * 8 : ENTH * 8 + 8, :] = done[x]
        if r == 0:
            store_strips(ENTH, state[MAIN:])
            last, first = pack_edges(state[MAIN:], 0, None, None)
            store_pack(1, 4, last, first)

    def tangents(r, q):
        last = first = None
        for it in range(4):
            j = q * 4 + it
            state = all_rows(r, j, q, it)
            for s in range(DEEP):
                def temp(i, s=s, state=state):
                    return sl[s * ALL + i] * state[i] + bump[(s * COEF + j) * ALL + i]

                state = advance(s, state, temp, *weights)
            done = merge(state)
            part = pl.ds(pl.multiple_of(j * 8, 8), 8)
            for x in range(8):
                mid[x, part, :] = done[x]
            if r == 0:
                store_strips(j, state[MAIN:])
                last, first = pack_edges(state[MAIN:], it, last, first)
        if r == 0:
            store_pack(1, q, last, first)

    enthalpy(0)
    for d in range(2):
        send_x(1, 4, d).start()
    for dx, dy in corners:
        send_p(1, 2, dx, dy).start()
    for group in range(2):
        for dx, dy in corners:
            send_p(0, group, dx, dy).wait()

    def first_round(q, _):
        for d in range(2):
            send_x(0, q, d).wait()
        tangents(0, q)
        for d in range(2):
            send_x(1, q, d).start()
        for group in range(2):
            @pl.when(q == 2 * group + 1)
            def _():
                for dx, dy in corners:
                    send_p(1, group, dx, dy).start()
        return 0

    lax.fori_loop(0, 4, first_round, 0)
    wait_e(1)
    enthalpy(1)

    def second_round(q, _):
        for group in range(2):
            @pl.when(q == 2 * group)
            def _():
                for dx, dy in corners:
                    send_p(1, group, dx, dy).wait()
        for d in range(2):
            send_x(1, q, d).wait()
        tangents(1, q)
        return 0

    lax.fori_loop(0, 4, second_round, 0)

    def top(item):
        v = jnp.broadcast_to(mid[0, item * 8 + 7 : item * 8 + 8, :], (8, 128))
        for x in range(1, 8):
            v = jnp.where(eight == x, mid[x, item * 8 + 7 : item * 8 + 8, :], v)
        return v

    p7 = jnp.where(lab_in[56:64, :] == 1, 1.0, 0.0) > 0
    scaled = jnp.where(p7, top(ENTH), 100.0) * (ROOT / WIDTH)
    slope = jnp.zeros((8, 128), F32)
    bumps = []
    for j in range(COEF):
        v = scaled - KNOTS[j] * (ROOT / WIDTH)
        b = jnp.exp2(-(v * v))
        bumps.append(b)
        slope = slope + v * (coef_in[j] * b)
    slope = jnp.where(p7, 1.0, 0.5) - (2.0 / (WIDTH * ROOT)) * slope
    for f in range(COEF):
        val = slope * top(f) + bumps[f]
        hi = val.astype(BF16).astype(F32)
        lo = val - hi
        for x in range(8):
            cols = slice(x * 128, (x + 1) * 128)
            at_k = atk[x]
            m_ref[f * MOST : (f + 1) * MOST, cols] = (at_k * hi[x : x + 1]).astype(BF16)
            m_ref[(COEF + f) * MOST : (COEF + f + 1) * MOST, cols] = (at_k * lo[x : x + 1]).astype(BF16)
    for g in range(4):
        hi = nt(a_ref[...], m_ref[g * 128 : (g + 1) * 128, :])
        lo = nt(a_ref[...], m_ref[512 + g * 128 : 512 + (g + 1) * 128, :])
        snd[g] = hi + lo

    pl.semaphore_wait(line_sem, len(line))
    mine = pl.ds(me, 1)
    keep = pltpu.make_async_copy(snd.at[:, mine, :], rcv.at[:, mine, :], local_sem)
    keep.start()

    def send_rows(i, _):
        t = lax.rem(me + i, n)
        pltpu.make_async_remote_copy(
            snd.at[:, pl.ds(t, 1), :], rcv.at[:, mine, :], all_send, all_recv,
            device_id=(t // n_gy, lax.rem(t, n_gy)), device_id_type=MESH,
        ).start()
        return 0

    lax.fori_loop(1, n, send_rows, 0)
    keep.wait()
    rest = pl.ds(0, n - 1)
    pltpu.make_async_remote_copy(
        snd.at[:, rest, :], rcv.at[:, rest, :], all_send, all_recv, device_id=at(1, 0), device_id_type=MESH
    ).wait()


def finish(mid, rcv, e_out, t_out, rows_out, e_tile, lhs, rhs, res, sem):
    def store_t(x):
        return pltpu.make_async_copy(mid.at[x, pl.ds(0, 128), :], t_out.at[:, x, :], sem.at[x])

    def store_e():
        return pltpu.make_async_copy(e_tile, e_out, sem.at[8])

    for x in range(8):
        store_t(x).start()
    for x in range(8):
        e_tile[pl.ds(x, 8, stride=8), :] = mid[x, ENTH * 8 : ENTH * 8 + 8, :]
    store_e().start()

    tall = lax.broadcasted_iota(jnp.int32, (128, 128), 0).astype(F32)
    eight = lax.broadcasted_iota(jnp.int32, (8, 128), 0).astype(F32)
    where = rcv[4].T
    vals = [rcv[g].T for g in range(4)]
    for k in range(MOST):
        cols = slice(k * 128, (k + 1) * 128)
        rhs[:, cols] = hot(tall, where[MOST + k : MOST + k + 1]).astype(BF16)
        at_hi = hot(eight + 1.0, where[k : k + 1])
        for f in range(COEF):
            at_f = (f % 4) * MOST + k
            lhs[f * 8 : f * 8 + 8, cols] = at_hi * vals[f // 4][at_f : at_f + 1]
    whole = lhs[...]
    hi = whole.astype(BF16)
    lo = (whole - hi.astype(F32)).astype(BF16)
    res[...] = nt(hi, rhs[...]) + nt(lo, rhs[...])
    for r in range(8):
        for half in range(2):
            rows_out[half * 8 : half * 8 + 8, r * 128 : (r + 1) * 128] = res[pl.ds(half * 64 + r, 8, stride=8), :]
    store_e().wait()
    for x in range(8):
        store_t(x).wait()


def solution(mesh):
    n_gx, n_gy = mesh.shape["gx"], mesh.shape["gy"]
    vmem = pl.BlockSpec(memory_space=pltpu.VMEM)
    hbm = pl.BlockSpec(memory_space=pltpu.HBM)
    dma = pltpu.SemaphoreType.DMA

    def in_hbm(x):
        return pltpu.with_memory_space_constraint(x, pltpu.HBM)

    def tiles(*shape):
        return pltpu.VMEM((*shape, 8, 128), F32)

    def local(enthalpy_start, tangent_start, labels, curve_parameters, pixel_cells, row_slot):
        mid, rcv = pl.pallas_call(
            functools.partial(kernel, n_gx, n_gy),
            out_shape=[
                jax.ShapeDtypeStruct((8, 136, 128), F32),
                jax.ShapeDtypeStruct((5, 128, 128), F32),
            ],
            in_specs=[hbm] * 6,
            out_specs=[vmem, vmem],
            scratch_shapes=[
                pltpu.VMEM((64, 128), F32),
                pltpu.VMEM((64, 128), jnp.int32),
                pltpu.VMEM((8, 128), jnp.int32),
                pltpu.VMEM((8, 128), jnp.int32),
                pltpu.SMEM((COEF,), F32),
                pltpu.VMEM((8, 144, 128), F32),
                pltpu.VMEM((2, DEEP, 144, 128), F32),
                pltpu.VMEM((2, DEEP, 136, 128), F32),
                pltpu.VMEM((ROUNDS, 2, 40, 128), F32),
                pltpu.VMEM((ROUNDS, 3, 2, 40, 128), F32),
                tiles((COEF + 2) * STRIP),
                tiles(2 * ALL),
                tiles(ALL),
                tiles(3 * ALL),
                tiles(DEEP * ALL),
                tiles(DEEP * COEF * ALL),
                pltpu.VMEM((128, 1024), BF16),
                pltpu.VMEM((8, MOST, 128), F32),
                pltpu.VMEM((128, 1024), BF16),
                pltpu.VMEM((1024, 1024), BF16),
                pltpu.VMEM((5, 128, 128), F32),
                dma((13,)),
                dma((ROUNDS, 5, 2)), dma((ROUNDS, 5, 2)),
                dma((ROUNDS, 3, 3, 2)), dma((ROUNDS, 3, 3, 2)),
                pltpu.SemaphoreType.REGULAR, dma, dma, dma,
            ],
            compiler_params=pltpu.CompilerParams(
                collective_id=0, has_side_effects=True, vmem_limit_bytes=40 * 2**20
            ),
            name="steps",
        )(
            in_hbm(enthalpy_start.reshape(64, 128)), in_hbm(tangent_start.reshape(128, 8, 128)),
            in_hbm(labels.reshape(64, 128)), in_hbm(curve_parameters),
            in_hbm(pixel_cells.reshape(8, 128)), in_hbm(row_slot.reshape(8, 128)),
        )
        e_end, t_end, rows = pl.pallas_call(
            finish,
            out_shape=[
                jax.ShapeDtypeStruct((64, 128), F32),
                jax.ShapeDtypeStruct((128, 8, 128), F32),
                jax.ShapeDtypeStruct((COEF, 1024), F32),
            ],
            in_specs=[vmem, vmem],
            out_specs=[hbm, hbm, vmem],
            scratch_shapes=[
                pltpu.VMEM((64, 128), F32),
                pltpu.VMEM((128, 4096), F32),
                pltpu.VMEM((128, 4096), BF16),
                pltpu.VMEM((128, 128), F32),
                dma((9,)),
            ],
            compiler_params=pltpu.CompilerParams(vmem_limit_bytes=40 * 2**20),
            name="finish",
        )(mid, rcv)
        return e_end.reshape(8, 8, 128), t_end.reshape(COEF, 8, 8, 128), rows

    in_specs = (
        P(None, "gx", "gy"),
        P(None, None, "gx", "gy"),
        P(None, "gx", "gy"),
        P(),
        P(("gx", "gy")),
        P(("gx", "gy")),
    )
    out_specs = (P(None, "gx", "gy"), P(None, None, "gx", "gy"), P(None, ("gx", "gy")))
    return jax.shard_map(local, mesh=mesh, in_specs=in_specs, out_specs=out_specs, check_vma=False)
```

```python
import functools
import math

import jax
import jax.numpy as jnp
from jax import lax
from jax.experimental import pallas as pl
from jax.experimental.pallas import tpu as pltpu
from jax.sharding import PartitionSpec as P

COEF = 16
RATE = 0.15
WIDTH = 0.3
ROOT = math.sqrt(math.log2(math.e))
KNOTS = [-2.0 + 0.25 * (j + 0.5) for j in range(COEF)]

DEEP = 4
ROUNDS = 2
MAIN = 16
STRIP = 4
ALL = MAIN + STRIP
ENTH = COEF
MOST = 32
GROUPS = ((0, 1, 2, 3),)
MESH = pl.DeviceIdType.MESH
F32 = jnp.float32
BF16 = jnp.bfloat16


def lanes():
    return lax.broadcasted_iota(jnp.int32, (8, 128), 1)


def turn(v, shift, axis):
    shift = shift % v.shape[axis]
    return v if shift == 0 else pltpu.roll(v, shift, axis)


def place(v, mask, piece):
    return piece if v is None else jnp.where(mask, piece, v)


def own_strips(rows):
    lane = lanes()
    out = []
    for g in range(STRIP):
        v = None
        for c in (1, 2):
            row = rows[4 * (c - 1) + g]
            v = place(v, lane // 16 == c, turn(row, 16 * c + 4, 1))
            v = place(v, lane // 16 == 4 + c, turn(row, 64 + 16 * c - 116, 1))
        out.append(v)
    return out


def pack_edges(strips, it, last, first):
    lane = lanes()
    for g in range(STRIP):
        here = (lane // 32 == g) & (lane % 16 // 4 == it)
        last = place(last, here, turn(strips[g], 32 * g + 4 * it - 88, 1))
        first = place(first, here, turn(strips[g], 32 * g + 4 * it - 20, 1))
    return last, first


def full_strips(own, low, high, before, after, it):
    lane = lanes()
    block, inside = lane // 16, lane % 16
    out = []
    for g in range(STRIP):
        v = own[g]
        v = place(v, block == 0, turn(low[g], 4, 1))
        v = place(v, block == 3, turn(high[g], 52, 1))
        v = place(v, block == 4, turn(low[g], -52, 1))
        v = place(v, block == 7, turn(high[g], -4, 1))
        at = 32 * g + 4 * it
        first, last = inside < 4, inside >= 12
        v = place(v, ((block == 1) | (block == 2)) & first, turn(before[1], 16 - at, 1))
        v = place(v, (block == 0) & first, turn(before[0], -16 - at, 1))
        v = place(v, (block == 3) & first, turn(before[2], 48 - at, 1))
        v = place(v, ((block == 5) | (block == 6)) & last, turn(after[1], 92 - at, 1))
        v = place(v, (block == 4) & last, turn(after[0], 60 - at, 1))
        v = place(v, (block == 7) & last, turn(after[2], 124 - at, 1))
        out.append(v)
    return out


def merge(state):
    lane = lanes()
    out = []
    for x in range(8):
        c, g = 1 + x // 4, x % 4
        v = jnp.where(lane < 4, turn(state[MAIN + g], -(16 * c + 4), 1), state[x + DEEP])
        out.append(jnp.where(lane >= 124, turn(state[MAIN + g], 124 - (72 + 16 * c), 1), v))
    return out


def advance(step, fields, load, store, temp, wx, wy, wz):
    def temps(i):
        olds = [load(k, i) for k in fields]
        return olds, [temp(k, i, v) for k, v in zip(fields, olds)]

    def across(i, ts, nexts):
        w = wx(i)
        return [w * (b - a) for a, b in zip(ts, nexts)]

    def update(i, olds, ts, fluxes, below):
        y, z = wy(i), wz(i)
        for k, old, t, flux, under in zip(fields, olds, ts, fluxes, below):
            fy = y * (turn(t, -1, 1) - t)
            fz = z * (turn(t, -1, 0) - t)
            store(k, i, old + ((flux - under) + ((fy - turn(fy, 1, 1)) + (fz - turn(fz, 1, 0)))))

    both = [temps(i) for i in range(MAIN, ALL)]
    ts = [t for _, t in both]
    ts.append([turn(t, -16, 1) for t in ts[0]])
    fluxes = [across(MAIN + g, ts[g], ts[g + 1]) for g in range(STRIP)]
    first = [turn(f, 16, 1) for f in fluxes[-1]]
    for g in range(STRIP):
        update(MAIN + g, *both[g], fluxes[g], fluxes[g - 1] if g > 0 else first)
    lo, hi = step, MAIN - step
    old, t = temps(lo)
    old_next, t_next = temps(lo + 1)
    flux = across(lo, t, t_next)
    for i in range(lo + 1, hi - 1):
        old, t = old_next, t_next
        old_next, t_next = temps(i + 1)
        below, flux = flux, across(i, t, t_next)
        update(i, old, t, flux, below)


def nt(a, b):
    return lax.dot_general(a, b, (((1,), (1,)), ((), ())), preferred_element_type=F32)


def hot(rows, row):
    return jnp.where(rows == row, 1.0, 0.0)


def kernel(
    n_gx, n_gy,
    e_ref, t_ref, lab_ref, coef_ref, cell_ref, slot_ref,
    mid, rcv,
    e_in, lab_in, cell_in, slot_in, coef_in, own, hx0, hx1, pk, hp, own_st, est, tst, fst, wst, sl, bump,
    a_ref, atk, tab, m_ref, snd,
    in_sem, x_send, x_recv, p_send, p_recv, line_sem, local_sem, all_send, all_recv,
):
    n = n_gx * n_gy
    gx, gy = lax.axis_index("gx"), lax.axis_index("gy")
    me = gx * n_gy + gy

    def at(dx, dy):
        return lax.rem(gx + dx + n_gx, n_gx), lax.rem(gy + dy + n_gy, n_gy)

    corners = [(dx, dy) for dx in (0, -1, 1) for dy in (-1, 1)]
    line = [(dx, 0) for dx in range(1, n_gx)]
    greeted = line + [(0, dy) for dy in range(1, n_gy)] + [c for c in corners if c[0] != 0]
    barrier = pltpu.get_barrier_semaphore()
    for dx, dy in greeted:
        pl.semaphore_signal(barrier, inc=1, device_id=at(dx, dy), device_id_type=MESH)

    def load_e():
        return pltpu.make_async_copy(e_ref, e_in, in_sem.at[8])

    def load_lab():
        return pltpu.make_async_copy(lab_ref, lab_in, in_sem.at[9])

    def load_t(x):
        return pltpu.make_async_copy(t_ref.at[:, x, :], own.at[x, pl.ds(0, 128), :], in_sem.at[x])

    def load_cell():
        return pltpu.make_async_copy(cell_ref, cell_in, in_sem.at[10])

    def load_slot():
        return pltpu.make_async_copy(slot_ref, slot_in, in_sem.at[11])

    def load_coef():
        return pltpu.make_async_copy(coef_ref, coef_in, in_sem.at[12])

    load_e().start()
    load_lab().start()
    for x in range(8):
        load_t(x).start()
    load_cell().start()
    load_slot().start()
    load_coef().start()
    load_e().wait()
    load_lab().wait()
    pair = [[], []]
    for x in range(8):
        pair[0].append(e_in[pl.ds(x, 8, stride=8), :])
        pair[1].append(jnp.where(lab_in[pl.ds(x, 8, stride=8), :] == 1, 1.0, 0.0))
        for k in range(2):
            own[x, (ENTH + k) * 8 : (ENTH + k + 1) * 8, :] = pair[k][x]

    halos = (hx0, hx1)

    def send_x(r, q, d):
        part = pl.ds(q * 32, 32) if not isinstance(q, int) or q < 4 else pl.ds(128, 16 if r == 0 else 8)
        source = own if r == 0 else mid
        return pltpu.make_async_remote_copy(
            source.at[pl.ds(DEEP - DEEP * d, DEEP), part, :], halos[r].at[d, :, part, :],
            x_send.at[r, q, d], x_recv.at[r, q, d], device_id=at(1 - 2 * d, 0), device_id_type=MESH,
        )

    def send_p(r, group, dx, dy):
        part = pl.ds(group * 16, 16) if group < 2 else pl.ds(32, 8)
        side = 0 if dy == 1 else 1
        return pltpu.make_async_remote_copy(
            pk.at[r, side, part], hp.at[r, 1 - dx, side, part],
            p_send.at[r, group, dx + 1, side], p_recv.at[r, group, 1 - dx, side],
            device_id=at(dx, dy), device_id_type=MESH,
        )

    def store_pack(r, q, last, first):
        to = pl.ds(pl.multiple_of(q * 8, 8), 8)
        pk[r, 0, to, :] = last
        pk[r, 1, to, :] = first

    def store_strips(item, strips):
        for g in range(STRIP):
            own_st[item * STRIP + g] = strips[g]

    last = first = None
    for k in range(2):
        strips = own_strips(pair[k])
        store_strips(ENTH + k, strips)
        last, first = pack_edges(strips, k, last, first)
    store_pack(0, 4, last, first)

    pl.semaphore_wait(barrier, len(greeted))
    for d in range(2):
        send_x(0, 4, d).start()
    for dx, dy in corners:
        send_p(0, 2, dx, dy).start()
    for dx, dy in line:
        pl.semaphore_signal(line_sem, inc=1, device_id=at(dx, dy), device_id_type=MESH)
    for x in range(8):
        load_t(x).wait()
    for d in range(2):
        send_x(0, 0, d).start()

    def own_rows(ref, item):
        part = pl.ds(pl.multiple_of(item * 8, 8), 8)
        return [ref[x, part, :] for x in range(8)]

    def pack_quad(q, _):
        last = first = None
        for it in range(4):
            strips = own_strips(own_rows(own, q * 4 + it))
            store_strips(q * 4 + it, strips)
            last, first = pack_edges(strips, it, last, first)
        store_pack(0, q, last, first)
        return 0

    lax.fori_loop(0, 4, pack_quad, 0)
    for group in range(2):
        for dx, dy in corners:
            send_p(0, group, dx, dy).start()
    for q in range(1, 4):
        for d in range(2):
            send_x(0, q, d).start()

    tall = lax.broadcasted_iota(jnp.int32, (128, 128), 0).astype(F32)
    wide = lax.broadcasted_iota(jnp.int32, (128, 128), 1).astype(F32)
    eight = lax.broadcasted_iota(jnp.int32, (8, 128), 0).astype(F32)
    load_cell().wait()
    load_slot().wait()
    load_coef().wait()
    cell, slot = cell_in[...], slot_in[...]
    owner = (slot // 1024).astype(F32)
    row = slot % 1024
    row_hi, row_lo = (row // 128 + 1).astype(F32), (row % 128).astype(F32)
    cell_x, cell_y = (cell // 128).astype(F32), (cell % 128).astype(F32)
    by_cell = jnp.zeros((24, 128), F32)
    for b in range(8):
        here = hot(eight, cell_x[b : b + 1])
        left = jnp.concatenate([here * w[b : b + 1] for w in (owner, row_hi, row_lo)], 0)
        by_cell = by_cell + nt(left.astype(BF16), hot(tall, cell_y[b : b + 1]).astype(BF16))
    owner, row_hi, row_lo = by_cell[0:8], by_cell[8:16], by_cell[16:24]
    earlier = jnp.where(tall < wide, 1.0, 0.0).astype(BF16)
    ones = jnp.ones((128, 128), BF16)
    seen = jnp.zeros((128, 128), F32)
    slot_k = lax.broadcasted_iota(jnp.int32, (MOST, 128), 0).astype(F32)
    for x in range(8):
        cols = slice(x * 128, (x + 1) * 128)
        mine = hot(tall, owner[x : x + 1])
        mine_b = mine.astype(BF16)
        a_ref[:, cols] = mine_b
        count = jnp.dot(mine_b, earlier, preferred_element_type=F32) + jnp.dot(
            seen.astype(BF16), ones, preferred_element_type=F32
        )
        seen = seen + mine
        at_k = hot(slot_k, jnp.sum(mine * count, axis=0, keepdims=True))
        atk[x] = at_k
        tab[0:MOST, cols] = (at_k * row_hi[x : x + 1]).astype(BF16)
        tab[MOST : 2 * MOST, cols] = (at_k * row_lo[x : x + 1]).astype(BF16)
        tab[2 * MOST : 4 * MOST, cols] = jnp.zeros((2 * MOST, 128), BF16)
    snd[4] = nt(a_ref[...], tab[...])

    def halo_rows(r, d, item):
        part = pl.ds(pl.multiple_of(item * 8, 8), 8)
        return [halos[r][d, x, part, :] for x in range(DEEP)]

    def all_rows(r, item, q, it):
        low, high = halo_rows(r, 0, item), halo_rows(r, 1, item)
        main = low + own_rows(own if r == 0 else mid, item) + high
        part = pl.ds(pl.multiple_of(q * 8, 8), 8)
        before = [hp[r, k, 0, part, :] for k in range(3)]
        after = [hp[r, k, 1, part, :] for k in range(3)]
        strips = [own_st[item * STRIP + g] for g in range(STRIP)]
        return main + full_strips(strips, low, high, before, after, it)

    def wait_e(r):
        for d in range(2):
            send_x(r, 4, d).wait()
        for dx, dy in corners:
            send_p(r, 2, dx, dy).wait()

    wait_e(0)
    pcm = all_rows(0, ENTH + 1, 4, 1)
    for i in range(ALL):
        est[ALL + i] = pcm[i]

    lane = lanes()
    block, inside = lane // 16, lane % 16
    layer = lax.broadcasted_iota(jnp.int32, (8, 128), 0)
    open_x0 = jnp.where(gx == 0, 0.0, 1.0)
    open_x1 = jnp.where(gx == n_gx - 1, 0.0, 1.0)
    open_y0 = jnp.where(gy == 0, 0.0, 1.0)
    open_y1 = jnp.where(gy == n_gy - 1, 0.0, 1.0)
    cond = [1.0 - 0.5 * p for p in pcm]

    def face(a, b):
        return (2.0 * RATE) * a * b / (a + b)

    edge_y = jnp.where((block < 4) & (inside == 3), open_y0, 1.0)
    edge_y = jnp.where((block >= 4) & (inside == 11), open_y1, edge_y)
    edge_x = jnp.where((block == 0) | (block == 4), open_x0, 1.0)
    edge_x = jnp.where((block == 2) | (block == 6), open_x1, edge_x)
    for i in range(ALL):
        c = cond[i]
        if i == MAIN - 1:
            up = c
        elif i == ALL - 1:
            up = turn(cond[MAIN], -16, 1)
        else:
            up = cond[i + 1]
        wx = face(c, up)
        if i == 3:
            wx = wx * open_x0
        if i == 11:
            wx = wx * open_x1
        if i == ALL - 1:
            wx = wx * edge_x
        wst[i] = wx
        wy = face(c, turn(c, -1, 1))
        wst[ALL + i] = wy * edge_y if i >= MAIN else wy
        wst[2 * ALL + i] = jnp.where(layer == 7, 0.0, face(c, turn(c, -1, 0)))

    weights = (lambda i: wst[i], lambda i: wst[ALL + i], lambda i: wst[2 * ALL + i])

    def shape_row(s, i):
        e = est[i]
        p = est[ALL + i] > 0
        scaled = jnp.where(p, e, 100.0) * (ROOT / WIDTH)
        total = jnp.zeros((8, 128), F32)
        slope = jnp.zeros((8, 128), F32)
        for j in range(COEF):
            v = scaled - KNOTS[j] * (ROOT / WIDTH)
            b = jnp.exp2(-(v * v))
            bump[(s * COEF + j) * ALL + i] = b
            cb = coef_in[j] * b
            total = total + cb
            slope = slope + v * cb
        half = jnp.where(p, 1.0, 0.5)
        tst[i] = half * e + total
        sl[s * ALL + i] = half - (2.0 / (WIDTH * ROOT)) * slope

    def shape_rows(s, lo, hi):
        for i in range(lo, lo + (hi - lo) % 4):
            shape_row(s, i)
        lo += (hi - lo) % 4

        def four(k, _):
            for i in range(4):
                shape_row(s, lo + k * 4 + i)
            return 0

        lax.fori_loop(0, (hi - lo) // 4, four, 0)

    def keep_e(k, i, v):
        est[i] = v

    def enthalpy(r):
        start = all_rows(r, ENTH, 4, 0)
        for i in range(ALL):
            est[i] = start[i]
        for s in range(DEEP):
            shape_rows(s, s, MAIN - s)
            shape_rows(s, MAIN, ALL)
            advance(s, [0], lambda k, i: est[i], keep_e, lambda k, i, v: tst[i], *weights)
        state = [est[i] for i in range(ALL)]
        done = merge(state)
        for x in range(8):
            mid[x, ENTH * 8 : ENTH * 8 + 8, :] = done[x]
        if r == 0:
            store_strips(ENTH, state[MAIN:])
            last, first = pack_edges(state[MAIN:], 0, None, None)
            store_pack(1, 4, last, first)

    def keep_t(k, i, v):
        fst[k * ALL + i] = v

    def tangents(r, q):
        last = first = None
        for its in GROUPS:
            for it in its:
                for i, v in enumerate(all_rows(r, q * 4 + it, q, it)):
                    fst[it * ALL + i] = v
            for s in range(DEEP):
                def temp(k, i, v, s=s):
                    return sl[s * ALL + i] * v + bump[(s * COEF + q * 4 + k) * ALL + i]

                advance(s, its, lambda k, i: fst[k * ALL + i], keep_t, temp, *weights)
            for it in its:
                j = q * 4 + it
                state = [fst[it * ALL + i] for i in range(ALL)]
                done = merge(state)
                part = pl.ds(pl.multiple_of(j * 8, 8), 8)
                for x in range(8):
                    mid[x, part, :] = done[x]
                if r == 0:
                    store_strips(j, state[MAIN:])
                    last, first = pack_edges(state[MAIN:], it, last, first)
        if r == 0:
            store_pack(1, q, last, first)

    enthalpy(0)
    for d in range(2):
        send_x(1, 4, d).start()
    for dx, dy in corners:
        send_p(1, 2, dx, dy).start()
    for group in range(2):
        for dx, dy in corners:
            send_p(0, group, dx, dy).wait()

    def first_round(q, _):
        for d in range(2):
            send_x(0, q, d).wait()
        tangents(0, q)
        for d in range(2):
            send_x(1, q, d).start()
        for group in range(2):
            @pl.when(q == 2 * group + 1)
            def _():
                for dx, dy in corners:
                    send_p(1, group, dx, dy).start()
        return 0

    lax.fori_loop(0, 4, first_round, 0)
    wait_e(1)
    enthalpy(1)

    def second_round(q, _):
        for group in range(2):
            @pl.when(q == 2 * group)
            def _():
                for dx, dy in corners:
                    send_p(1, group, dx, dy).wait()
        for d in range(2):
            send_x(1, q, d).wait()
        tangents(1, q)
        return 0

    lax.fori_loop(0, 4, second_round, 0)

    def top(item):
        v = jnp.broadcast_to(mid[0, item * 8 + 7 : item * 8 + 8, :], (8, 128))
        for x in range(1, 8):
            v = jnp.where(eight == x, mid[x, item * 8 + 7 : item * 8 + 8, :], v)
        return v

    p7 = jnp.where(lab_in[56:64, :] == 1, 1.0, 0.0) > 0
    scaled = jnp.where(p7, top(ENTH), 100.0) * (ROOT / WIDTH)
    slope = jnp.zeros((8, 128), F32)
    bumps = []
    for j in range(COEF):
        v = scaled - KNOTS[j] * (ROOT / WIDTH)
        b = jnp.exp2(-(v * v))
        bumps.append(b)
        slope = slope + v * (coef_in[j] * b)
    slope = jnp.where(p7, 1.0, 0.5) - (2.0 / (WIDTH * ROOT)) * slope
    for f in range(COEF):
        val = slope * top(f) + bumps[f]
        hi = val.astype(BF16).astype(F32)
        lo = val - hi
        for x in range(8):
            cols = slice(x * 128, (x + 1) * 128)
            at_k = atk[x]
            m_ref[f * MOST : (f + 1) * MOST, cols] = (at_k * hi[x : x + 1]).astype(BF16)
            m_ref[(COEF + f) * MOST : (COEF + f + 1) * MOST, cols] = (at_k * lo[x : x + 1]).astype(BF16)
    for g in range(4):
        hi = nt(a_ref[...], m_ref[g * 128 : (g + 1) * 128, :])
        lo = nt(a_ref[...], m_ref[512 + g * 128 : 512 + (g + 1) * 128, :])
        snd[g] = hi + lo

    pl.semaphore_wait(line_sem, len(line))
    mine = pl.ds(me, 1)
    keep = pltpu.make_async_copy(snd.at[:, mine, :], rcv.at[:, mine, :], local_sem)
    keep.start()

    def send_rows(i, _):
        t = lax.rem(me + i, n)
        pltpu.make_async_remote_copy(
            snd.at[:, pl.ds(t, 1), :], rcv.at[:, mine, :], all_send, all_recv,
            device_id=(t // n_gy, lax.rem(t, n_gy)), device_id_type=MESH,
        ).start()
        return 0

    lax.fori_loop(1, n, send_rows, 0)
    keep.wait()
    rest = pl.ds(0, n - 1)
    pltpu.make_async_remote_copy(
        snd.at[:, rest, :], rcv.at[:, rest, :], all_send, all_recv, device_id=at(1, 0), device_id_type=MESH
    ).wait()


def finish(mid, rcv, e_out, t_out, rows_out, e_tile, lhs, rhs, res, sem):
    def store_t(x):
        return pltpu.make_async_copy(mid.at[x, pl.ds(0, 128), :], t_out.at[:, x, :], sem.at[x])

    def store_e():
        return pltpu.make_async_copy(e_tile, e_out, sem.at[8])

    for x in range(8):
        store_t(x).start()
    for x in range(8):
        e_tile[pl.ds(x, 8, stride=8), :] = mid[x, ENTH * 8 : ENTH * 8 + 8, :]
    store_e().start()

    tall = lax.broadcasted_iota(jnp.int32, (128, 128), 0).astype(F32)
    eight = lax.broadcasted_iota(jnp.int32, (8, 128), 0).astype(F32)
    where = rcv[4].T
    vals = [rcv[g].T for g in range(4)]
    for k in range(MOST):
        cols = slice(k * 128, (k + 1) * 128)
        rhs[:, cols] = hot(tall, where[MOST + k : MOST + k + 1]).astype(BF16)
        at_hi = hot(eight + 1.0, where[k : k + 1])
        for f in range(COEF):
            at_f = (f % 4) * MOST + k
            lhs[f * 8 : f * 8 + 8, cols] = at_hi * vals[f // 4][at_f : at_f + 1]
    whole = lhs[...]
    hi = whole.astype(BF16)
    lo = (whole - hi.astype(F32)).astype(BF16)
    res[...] = nt(hi, rhs[...]) + nt(lo, rhs[...])
    for r in range(8):
        for half in range(2):
            rows_out[half * 8 : half * 8 + 8, r * 128 : (r + 1) * 128] = res[pl.ds(half * 64 + r, 8, stride=8), :]
    store_e().wait()
    for x in range(8):
        store_t(x).wait()


def solution(mesh):
    n_gx, n_gy = mesh.shape["gx"], mesh.shape["gy"]
    vmem = pl.BlockSpec(memory_space=pltpu.VMEM)
    hbm = pl.BlockSpec(memory_space=pltpu.HBM)
    dma = pltpu.SemaphoreType.DMA

    def in_hbm(x):
        return pltpu.with_memory_space_constraint(x, pltpu.HBM)

    def tiles(*shape):
        return pltpu.VMEM((*shape, 8, 128), F32)

    def local(enthalpy_start, tangent_start, labels, curve_parameters, pixel_cells, row_slot):
        mid, rcv = pl.pallas_call(
            functools.partial(kernel, n_gx, n_gy),
            out_shape=[
                jax.ShapeDtypeStruct((8, 136, 128), F32),
                jax.ShapeDtypeStruct((5, 128, 128), F32),
            ],
            in_specs=[hbm] * 6,
            out_specs=[vmem, vmem],
            scratch_shapes=[
                pltpu.VMEM((64, 128), F32),
                pltpu.VMEM((64, 128), jnp.int32),
                pltpu.VMEM((8, 128), jnp.int32),
                pltpu.VMEM((8, 128), jnp.int32),
                pltpu.SMEM((COEF,), F32),
                pltpu.VMEM((8, 144, 128), F32),
                pltpu.VMEM((2, DEEP, 144, 128), F32),
                pltpu.VMEM((2, DEEP, 136, 128), F32),
                pltpu.VMEM((ROUNDS, 2, 40, 128), F32),
                pltpu.VMEM((ROUNDS, 3, 2, 40, 128), F32),
                tiles((COEF + 2) * STRIP),
                tiles(2 * ALL),
                tiles(ALL),
                tiles(4 * ALL),
                tiles(3 * ALL),
                tiles(DEEP * ALL),
                tiles(DEEP * COEF * ALL),
                pltpu.VMEM((128, 1024), BF16),
                pltpu.VMEM((8, MOST, 128), F32),
                pltpu.VMEM((128, 1024), BF16),
                pltpu.VMEM((1024, 1024), BF16),
                pltpu.VMEM((5, 128, 128), F32),
                dma((13,)),
                dma((ROUNDS, 5, 2)), dma((ROUNDS, 5, 2)),
                dma((ROUNDS, 3, 3, 2)), dma((ROUNDS, 3, 3, 2)),
                pltpu.SemaphoreType.REGULAR, dma, dma, dma,
            ],
            compiler_params=pltpu.CompilerParams(
                collective_id=0, has_side_effects=True, vmem_limit_bytes=40 * 2**20
            ),
            name="steps",
        )(
            in_hbm(enthalpy_start.reshape(64, 128)), in_hbm(tangent_start.reshape(128, 8, 128)),
            in_hbm(labels.reshape(64, 128)), in_hbm(curve_parameters),
            in_hbm(pixel_cells.reshape(8, 128)), in_hbm(row_slot.reshape(8, 128)),
        )
        e_end, t_end, rows = pl.pallas_call(
            finish,
            out_shape=[
                jax.ShapeDtypeStruct((64, 128), F32),
                jax.ShapeDtypeStruct((128, 8, 128), F32),
                jax.ShapeDtypeStruct((COEF, 1024), F32),
            ],
            in_specs=[vmem, vmem],
            out_specs=[hbm, hbm, vmem],
            scratch_shapes=[
                pltpu.VMEM((64, 128), F32),
                pltpu.VMEM((128, 4096), F32),
                pltpu.VMEM((128, 4096), BF16),
                pltpu.VMEM((128, 128), F32),
                dma((9,)),
            ],
            compiler_params=pltpu.CompilerParams(vmem_limit_bytes=40 * 2**20),
            name="finish",
        )(mid, rcv)
        return e_end.reshape(8, 8, 128), t_end.reshape(COEF, 8, 8, 128), rows

    in_specs = (
        P(None, "gx", "gy"),
        P(None, None, "gx", "gy"),
        P(None, "gx", "gy"),
        P(),
        P(("gx", "gy")),
        P(("gx", "gy")),
    )
    out_specs = (P(None, "gx", "gy"), P(None, None, "gx", "gy"), P(None, ("gx", "gy")))
    return jax.shard_map(local, mesh=mesh, in_specs=in_specs, out_specs=out_specs, check_vma=False)
```

```python
import functools
import math

import jax
import jax.numpy as jnp
from jax import lax
from jax.experimental import pallas as pl
from jax.experimental.pallas import tpu as pltpu
from jax.sharding import PartitionSpec as P

COEF = 16
RATE = 0.15
WIDTH = 0.3
ROOT = math.sqrt(math.log2(math.e))
KNOTS = [-2.0 + 0.25 * (j + 0.5) for j in range(COEF)]

DEEP = 4
ROUNDS = 2
MAIN = 16
STRIP = 4
ALL = MAIN + STRIP
ENTH = COEF
MOST = 32
GROUPS = ((0, 1, 2, 3),)
MESH = pl.DeviceIdType.MESH
F32 = jnp.float32
BF16 = jnp.bfloat16


def lanes():
    return lax.broadcasted_iota(jnp.int32, (8, 128), 1)


def turn(v, shift, axis):
    shift = shift % v.shape[axis]
    return v if shift == 0 else pltpu.roll(v, shift, axis)


def place(v, mask, piece):
    return piece if v is None else jnp.where(mask, piece, v)


def own_strips(rows):
    lane = lanes()
    out = []
    for g in range(STRIP):
        v = None
        for c in (1, 2):
            row = rows[4 * (c - 1) + g]
            v = place(v, lane // 16 == c, turn(row, 16 * c + 4, 1))
            v = place(v, lane // 16 == 4 + c, turn(row, 64 + 16 * c - 116, 1))
        out.append(v)
    return out


def pack_edges(strips, it, last, first):
    lane = lanes()
    for g in range(STRIP):
        here = (lane // 32 == g) & (lane % 16 // 4 == it)
        last = place(last, here, turn(strips[g], 32 * g + 4 * it - 88, 1))
        first = place(first, here, turn(strips[g], 32 * g + 4 * it - 20, 1))
    return last, first


def widen(edges):
    lane = lanes()
    low, own, high = edges
    out = []
    for h in range(2):
        v = None
        for g in (2 * h, 2 * h + 1):
            base = 64 * (g % 2)
            v = place(v, (lane >= base + 16) & (lane < base + 48), turn(own, base + 16 - 32 * g, 1))
            v = place(v, lane // 16 == base // 16, turn(low, base - 16 - 32 * g, 1))
            v = place(v, lane // 16 == base // 16 + 3, turn(high, base + 48 - 32 * g, 1))
        out.append(v)
    return out


def full_strips(own, low, high, before, after, it):
    lane = lanes()
    block, inside = lane // 16, lane % 16
    out = []
    for g in range(STRIP):
        v = own[g]
        v = place(v, block == 0, turn(low[g], 4, 1))
        v = place(v, block == 3, turn(high[g], 52, 1))
        v = place(v, block == 4, turn(low[g], -52, 1))
        v = place(v, block == 7, turn(high[g], -4, 1))
        at = 64 * (g % 2) + 4 * it
        v = place(v, (block < 4) & (inside < 4), turn(before[g // 2], -at, 1))
        v = place(v, (block >= 4) & (inside >= 12), turn(after[g // 2], 76 - at, 1))
        out.append(v)
    return out


def merge(state):
    lane = lanes()
    out = []
    for x in range(8):
        c, g = 1 + x // 4, x % 4
        v = jnp.where(lane < 4, turn(state[MAIN + g], -(16 * c + 4), 1), state[x + DEEP])
        out.append(jnp.where(lane >= 124, turn(state[MAIN + g], 124 - (72 + 16 * c), 1), v))
    return out


def advance(step, fields, load, store, temp, wx, wy, wz):
    def temps(i):
        olds = [load(k, i) for k in fields]
        return olds, [temp(k, i, v) for k, v in zip(fields, olds)]

    def across(i, ts, nexts):
        w = wx(i)
        return [w * (b - a) for a, b in zip(ts, nexts)]

    def update(i, olds, ts, fluxes, below):
        y, z = wy(i), wz(i)
        for k, old, t, flux, under in zip(fields, olds, ts, fluxes, below):
            fy = y * (turn(t, -1, 1) - t)
            fz = z * (turn(t, -1, 0) - t)
            store(k, i, old + ((flux - under) + ((fy - turn(fy, 1, 1)) + (fz - turn(fz, 1, 0)))))

    both = [temps(i) for i in range(MAIN, ALL)]
    ts = [t for _, t in both]
    ts.append([turn(t, -16, 1) for t in ts[0]])
    fluxes = [across(MAIN + g, ts[g], ts[g + 1]) for g in range(STRIP)]
    first = [turn(f, 16, 1) for f in fluxes[-1]]
    for g in range(STRIP):
        update(MAIN + g, *both[g], fluxes[g], fluxes[g - 1] if g > 0 else first)
    lo, hi = step, MAIN - step
    old, t = temps(lo)
    old_next, t_next = temps(lo + 1)
    flux = across(lo, t, t_next)
    for i in range(lo + 1, hi - 1):
        old, t = old_next, t_next
        old_next, t_next = temps(i + 1)
        below, flux = flux, across(i, t, t_next)
        update(i, old, t, flux, below)


def nt(a, b):
    return lax.dot_general(a, b, (((1,), (1,)), ((), ())), preferred_element_type=F32)


def hot(rows, row):
    return jnp.where(rows == row, 1.0, 0.0)


def kernel(
    n_gx, n_gy,
    e_ref, t_ref, lab_ref, coef_ref, cell_ref, slot_ref,
    mid, rcv,
    e_in, lab_in, cell_in, slot_in, coef_in, own, hx0, hx1, pk, hp, own_st, est, tst, fst, wst, sl, bump,
    a_ref, atk, tab, m_ref, top_st, snd,
    in_sem, x_send, x_recv, p_send, p_recv, near_sem, local_sem, all_send, all_recv,
):
    n = n_gx * n_gy
    gx, gy = lax.axis_index("gx"), lax.axis_index("gy")
    me = gx * n_gy + gy

    def at(dx, dy):
        return lax.rem(gx + dx + n_gx, n_gx), lax.rem(gy + dy + n_gy, n_gy)

    corners = [(dx, dy) for dx in (0, -1, 1) for dy in (-1, 1)]
    around = corners + [(-1, 0), (1, 0)]
    rounds = [around, [(2 * dx, 2 * dy) for dx, dy in around], [(-4, 0), (4, 0)]]

    def greet(k):
        for dx, dy in rounds[k]:
            pl.semaphore_signal(near_sem.at[k], inc=1, device_id=at(dx, dy), device_id_type=MESH)

    def greeted(k):
        pl.semaphore_wait(near_sem.at[k], len(rounds[k]))

    barrier = pltpu.get_barrier_semaphore()
    for dx, dy in around:
        pl.semaphore_signal(barrier, inc=1, device_id=at(dx, dy), device_id_type=MESH)

    def load_e():
        return pltpu.make_async_copy(e_ref, e_in, in_sem.at[8])

    def load_lab():
        return pltpu.make_async_copy(lab_ref, lab_in, in_sem.at[9])

    def load_t(x):
        return pltpu.make_async_copy(t_ref.at[:, x, :], own.at[x, pl.ds(0, 128), :], in_sem.at[x])

    def load_cell():
        return pltpu.make_async_copy(cell_ref, cell_in, in_sem.at[10])

    def load_slot():
        return pltpu.make_async_copy(slot_ref, slot_in, in_sem.at[11])

    def load_coef():
        return pltpu.make_async_copy(coef_ref, coef_in, in_sem.at[12])

    load_e().start()
    load_lab().start()
    for x in range(8):
        load_t(x).start()
    load_cell().start()
    load_slot().start()
    load_coef().start()
    load_e().wait()
    load_lab().wait()
    pair = [[], []]
    for x in range(8):
        pair[0].append(e_in[pl.ds(x, 8, stride=8), :])
        pair[1].append(jnp.where(lab_in[pl.ds(x, 8, stride=8), :] == 1, 1.0, 0.0))
        for k in range(2):
            own[x, (ENTH + k) * 8 : (ENTH + k + 1) * 8, :] = pair[k][x]

    halos = (hx0, hx1)

    def send_x(r, q, d):
        part = pl.ds(q * 32, 32) if not isinstance(q, int) or q < 4 else pl.ds(128, 16 if r == 0 else 8)
        source = own if r == 0 else mid
        return pltpu.make_async_remote_copy(
            source.at[pl.ds(DEEP - DEEP * d, DEEP), part, :], halos[r].at[d, :, part, :],
            x_send.at[r, q, d], x_recv.at[r, q, d], device_id=at(1 - 2 * d, 0), device_id_type=MESH,
        )

    def send_p(r, group, dx, dy):
        part = pl.ds(group * 16, 16) if group < 2 else pl.ds(32, 8)
        side = 0 if dy == 1 else 1
        return pltpu.make_async_remote_copy(
            pk.at[r, side, part], hp.at[r, 1 - dx, side, part],
            p_send.at[r, group, dx + 1, side], p_recv.at[r, group, 1 - dx, side],
            device_id=at(dx, dy), device_id_type=MESH,
        )

    def store_pack(r, q, last, first):
        to = pl.ds(pl.multiple_of(q * 8, 8), 8)
        pk[r, 0, to, :] = last
        pk[r, 1, to, :] = first

    def store_strips(item, strips):
        for g in range(STRIP):
            own_st[item * STRIP + g] = strips[g]

    last = first = None
    for k in range(2):
        strips = own_strips(pair[k])
        store_strips(ENTH + k, strips)
        last, first = pack_edges(strips, k, last, first)
    store_pack(0, 4, last, first)

    pl.semaphore_wait(barrier, len(around))
    for d in range(2):
        send_x(0, 4, d).start()
    for dx, dy in corners:
        send_p(0, 2, dx, dy).start()
    for x in range(8):
        load_t(x).wait()
    for d in range(2):
        send_x(0, 0, d).start()

    def own_rows(ref, item):
        part = pl.ds(pl.multiple_of(item * 8, 8), 8)
        return [ref[x, part, :] for x in range(8)]

    def pack_quad(q, _):
        last = first = None
        for it in range(4):
            strips = own_strips(own_rows(own, q * 4 + it))
            store_strips(q * 4 + it, strips)
            last, first = pack_edges(strips, it, last, first)
        store_pack(0, q, last, first)
        return 0

    lax.fori_loop(0, 4, pack_quad, 0)
    for group in range(2):
        for dx, dy in corners:
            send_p(0, group, dx, dy).start()
    for q in range(1, 4):
        for d in range(2):
            send_x(0, q, d).start()

    greet(0)

    tall = lax.broadcasted_iota(jnp.int32, (128, 128), 0).astype(F32)
    wide = lax.broadcasted_iota(jnp.int32, (128, 128), 1).astype(F32)
    eight = lax.broadcasted_iota(jnp.int32, (8, 128), 0).astype(F32)
    load_cell().wait()
    load_slot().wait()
    load_coef().wait()
    cell, slot = cell_in[...], slot_in[...]
    owner = (slot // 1024).astype(F32)
    row = slot % 1024
    row_hi, row_lo = (row // 128 + 1).astype(F32), (row % 128).astype(F32)
    cell_x, cell_y = (cell // 128).astype(F32), (cell % 128).astype(F32)
    by_cell = jnp.zeros((24, 128), F32)
    for b in range(8):
        here = hot(eight, cell_x[b : b + 1])
        left = jnp.concatenate([here * w[b : b + 1] for w in (owner, row_hi, row_lo)], 0)
        by_cell = by_cell + nt(left.astype(BF16), hot(tall, cell_y[b : b + 1]).astype(BF16))
    owner, row_hi, row_lo = by_cell[0:8], by_cell[8:16], by_cell[16:24]
    earlier = jnp.where(tall < wide, 1.0, 0.0).astype(BF16)
    ones = jnp.ones((128, 128), BF16)
    seen = jnp.zeros((128, 128), F32)
    slot_k = lax.broadcasted_iota(jnp.int32, (MOST, 128), 0).astype(F32)
    for x in range(8):
        cols = slice(x * 128, (x + 1) * 128)
        mine = hot(tall, owner[x : x + 1])
        mine_b = mine.astype(BF16)
        a_ref[:, cols] = mine_b
        count = jnp.dot(mine_b, earlier, preferred_element_type=F32) + jnp.dot(
            seen.astype(BF16), ones, preferred_element_type=F32
        )
        seen = seen + mine
        at_k = hot(slot_k, jnp.sum(mine * count, axis=0, keepdims=True))
        atk[x] = at_k
        tab[0:MOST, cols] = (at_k * row_hi[x : x + 1]).astype(BF16)
        tab[MOST : 2 * MOST, cols] = (at_k * row_lo[x : x + 1]).astype(BF16)
        tab[2 * MOST : 4 * MOST, cols] = jnp.zeros((2 * MOST, 128), BF16)
    snd[4] = nt(a_ref[...], tab[...])

    def shape_row(r, s, i):
        e = est[i]
        p = est[ALL + i] > 0
        scaled = jnp.where(p, e, 100.0) * (ROOT / WIDTH)
        total = jnp.zeros((8, 128), F32)
        slope = jnp.zeros((8, 128), F32)
        for j in range(COEF):
            v = scaled - KNOTS[j] * (ROOT / WIDTH)
            b = jnp.exp2(-(v * v))
            bump[((r * DEEP + s) * COEF + j) * ALL + i] = b
            cb = coef_in[j] * b
            total = total + cb
            slope = slope + v * cb
        half = jnp.where(p, 1.0, 0.5)
        tst[i] = half * e + total
        sl[(r * DEEP + s) * ALL + i] = half - (2.0 / (WIDTH * ROOT)) * slope

    def shape_rows(r, s, lo, hi):
        for i in range(lo, lo + (hi - lo) % 4):
            shape_row(r, s, i)
        lo += (hi - lo) % 4

        def four(k, _):
            for i in range(4):
                shape_row(r, s, lo + k * 4 + i)
            return 0

        lax.fori_loop(0, (hi - lo) // 4, four, 0)

    def halo_rows(r, d, item):
        part = pl.ds(pl.multiple_of(item * 8, 8), 8)
        return [halos[r][d, x, part, :] for x in range(DEEP)]

    def wide_edges(r, q):
        part = pl.ds(pl.multiple_of(q * 8, 8), 8)
        return [widen([hp[r, k, side, part, :] for k in range(3)]) for side in range(2)]

    def all_rows(r, item, wide, it):
        low, high = halo_rows(r, 0, item), halo_rows(r, 1, item)
        main = low + own_rows(own if r == 0 else mid, item) + high
        strips = [own_st[item * STRIP + g] for g in range(STRIP)]
        return main + full_strips(strips, low, high, *wide, it)

    def wait_e(r):
        for d in range(2):
            send_x(r, 4, d).wait()
        for dx, dy in corners:
            send_p(r, 2, dx, dy).wait()

    for x in range(8):
        est[DEEP + x] = own[x, ENTH * 8 : ENTH * 8 + 8, :]
        est[ALL + DEEP + x] = own[x, (ENTH + 1) * 8 : (ENTH + 2) * 8, :]
    shape_rows(0, 0, DEEP, MAIN - DEEP)
    wait_e(0)
    pcm = all_rows(0, ENTH + 1, wide_edges(0, 4), 1)
    for i in range(ALL):
        est[ALL + i] = pcm[i]

    lane = lanes()
    block, inside = lane // 16, lane % 16
    layer = lax.broadcasted_iota(jnp.int32, (8, 128), 0)
    open_x0 = jnp.where(gx == 0, 0.0, 1.0)
    open_x1 = jnp.where(gx == n_gx - 1, 0.0, 1.0)
    open_y0 = jnp.where(gy == 0, 0.0, 1.0)
    open_y1 = jnp.where(gy == n_gy - 1, 0.0, 1.0)
    cond = [1.0 - 0.5 * p for p in pcm]

    def face(a, b):
        return (2.0 * RATE) * a * b / (a + b)

    edge_y = jnp.where((block < 4) & (inside == 3), open_y0, 1.0)
    edge_y = jnp.where((block >= 4) & (inside == 11), open_y1, edge_y)
    edge_x = jnp.where((block == 0) | (block == 4), open_x0, 1.0)
    edge_x = jnp.where((block == 2) | (block == 6), open_x1, edge_x)
    for i in range(ALL):
        c = cond[i]
        if i == MAIN - 1:
            up = c
        elif i == ALL - 1:
            up = turn(cond[MAIN], -16, 1)
        else:
            up = cond[i + 1]
        wx = face(c, up)
        if i == 3:
            wx = wx * open_x0
        if i == 11:
            wx = wx * open_x1
        if i == ALL - 1:
            wx = wx * edge_x
        wst[i] = wx
        wy = face(c, turn(c, -1, 1))
        wst[ALL + i] = wy * edge_y if i >= MAIN else wy
        wst[2 * ALL + i] = jnp.where(layer == 7, 0.0, face(c, turn(c, -1, 0)))

    weights = (lambda i: wst[i], lambda i: wst[ALL + i], lambda i: wst[2 * ALL + i])

    def keep_e(k, i, v):
        est[i] = v

    def enthalpy(r):
        start = all_rows(r, ENTH, wide_edges(r, 4), 0)
        for i in range(ALL):
            est[i] = start[i]
        for s in range(DEEP):
            if r == 0 and s == 0:
                shape_rows(r, s, 0, DEEP)
                shape_rows(r, s, MAIN - DEEP, ALL)
            else:
                shape_rows(r, s, s, MAIN - s)
                shape_rows(r, s, MAIN, ALL)
            advance(s, [0], lambda k, i: est[i], keep_e, lambda k, i, v: tst[i], *weights)
        state = [est[i] for i in range(ALL)]
        done = merge(state)
        for x in range(8):
            mid[x, ENTH * 8 : ENTH * 8 + 8, :] = done[x]
        if r == 0:
            store_strips(ENTH, state[MAIN:])
            last, first = pack_edges(state[MAIN:], 0, None, None)
            store_pack(1, 4, last, first)

    def keep_t(k, i, v):
        fst[k * ALL + i] = v

    def tangents(r, q):
        last = first = None
        wide = wide_edges(r, q)
        for its in GROUPS:
            for it in its:
                for i, v in enumerate(all_rows(r, q * 4 + it, wide, it)):
                    fst[it * ALL + i] = v
            for s in range(DEEP):
                def temp(k, i, v, s=s):
                    return sl[(r * DEEP + s) * ALL + i] * v + bump[((r * DEEP + s) * COEF + q * 4 + k) * ALL + i]

                advance(s, its, lambda k, i: fst[k * ALL + i], keep_t, temp, *weights)
            for it in its:
                j = q * 4 + it
                state = [fst[it * ALL + i] for i in range(ALL)]
                done = merge(state)
                part = pl.ds(pl.multiple_of(j * 8, 8), 8)
                for x in range(8):
                    mid[x, part, :] = done[x]
                if r == 0:
                    store_strips(j, state[MAIN:])
                    last, first = pack_edges(state[MAIN:], it, last, first)
        if r == 0:
            store_pack(1, q, last, first)

    enthalpy(0)
    greeted(0)
    greet(1)
    for d in range(2):
        send_x(1, 4, d).start()
    for dx, dy in corners:
        send_p(1, 2, dx, dy).start()
    for group in range(2):
        for dx, dy in corners:
            send_p(0, group, dx, dy).wait()

    def first_round(q, _):
        for d in range(2):
            send_x(0, q, d).wait()
        tangents(0, q)
        for group in range(2):
            @pl.when(q == 2 * group + 1)
            def _():
                for dx, dy in corners:
                    send_p(1, group, dx, dy).start()
        for d in range(2):
            send_x(1, q, d).start()
        return 0

    lax.fori_loop(0, 4, first_round, 0)
    greeted(1)
    greet(2)
    wait_e(1)
    enthalpy(1)

    def top(item):
        v = jnp.broadcast_to(mid[0, pl.ds(item * 8 + 7, 1), :], (8, 128))
        for x in range(1, 8):
            v = jnp.where(eight == x, mid[x, pl.ds(item * 8 + 7, 1), :], v)
        return v

    p7 = jnp.where(lab_in[56:64, :] == 1, 1.0, 0.0) > 0
    scaled = jnp.where(p7, top(ENTH), 100.0) * (ROOT / WIDTH)
    slope = jnp.zeros((8, 128), F32)
    for j in range(COEF):
        v = scaled - KNOTS[j] * (ROOT / WIDTH)
        b = jnp.exp2(-(v * v))
        top_st[j] = b
        slope = slope + v * (coef_in[j] * b)
    top_st[COEF] = jnp.where(p7, 1.0, 0.5) - (2.0 / (WIDTH * ROOT)) * slope

    def pack_rows(q):
        for it in range(4):
            f = q * 4 + it
            val = top_st[COEF] * top(f) + top_st[f]
            hi = val.astype(BF16).astype(F32)
            lo = val - hi
            for x in range(8):
                cols = slice(x * 128, (x + 1) * 128)
                at_k = atk[x]
                m_ref[it * MOST : (it + 1) * MOST, cols] = (at_k * hi[x : x + 1]).astype(BF16)
                m_ref[128 + it * MOST : 128 + (it + 1) * MOST, cols] = (at_k * lo[x : x + 1]).astype(BF16)
        both = nt(a_ref[...], m_ref[...])
        snd[q] = both[:, :128] + both[:, 128:]

    def second_round(q, _):
        for group in range(2):
            @pl.when(q == 2 * group)
            def _():
                for dx, dy in corners:
                    send_p(1, group, dx, dy).wait()
        for d in range(2):
            send_x(1, q, d).wait()
        tangents(1, q)
        pack_rows(q)
        return 0

    lax.fori_loop(0, 4, second_round, 0)

    greeted(2)
    mine = pl.ds(me, 1)
    keep = pltpu.make_async_copy(snd.at[:, mine, :], rcv.at[:, mine, :], local_sem)
    keep.start()

    def send_rows(i, _):
        t = lax.rem(me + i, n)
        pltpu.make_async_remote_copy(
            snd.at[:, pl.ds(t, 1), :], rcv.at[:, mine, :], all_send, all_recv,
            device_id=(t // n_gy, lax.rem(t, n_gy)), device_id_type=MESH,
        ).start()
        return 0

    lax.fori_loop(1, n, send_rows, 0)
    keep.wait()
    rest = pl.ds(0, n - 1)
    pltpu.make_async_remote_copy(
        snd.at[:, rest, :], rcv.at[:, rest, :], all_send, all_recv, device_id=at(1, 0), device_id_type=MESH
    ).wait()


def finish(mid, rcv, e_out, t_out, rows_out, e_tile, lhs, rhs, res, sem):
    def store_t(x):
        return pltpu.make_async_copy(mid.at[x, pl.ds(0, 128), :], t_out.at[:, x, :], sem.at[x])

    def store_e():
        return pltpu.make_async_copy(e_tile, e_out, sem.at[8])

    for x in range(8):
        store_t(x).start()
    for x in range(8):
        e_tile[pl.ds(x, 8, stride=8), :] = mid[x, ENTH * 8 : ENTH * 8 + 8, :]
    store_e().start()

    tall = lax.broadcasted_iota(jnp.int32, (128, 128), 0).astype(F32)
    eight = lax.broadcasted_iota(jnp.int32, (8, 128), 0).astype(F32)
    where = rcv[4].T
    vals = [rcv[g].T for g in range(4)]
    for k in range(MOST):
        cols = slice(k * 128, (k + 1) * 128)
        rhs[:, cols] = hot(tall, where[MOST + k : MOST + k + 1]).astype(BF16)
        at_hi = hot(eight + 1.0, where[k : k + 1])
        for f in range(COEF):
            at_f = (f % 4) * MOST + k
            lhs[f * 8 : f * 8 + 8, cols] = at_hi * vals[f // 4][at_f : at_f + 1]
    whole = lhs[...]
    hi = whole.astype(BF16)
    lo = (whole - hi.astype(F32)).astype(BF16)
    both = nt(jnp.concatenate([hi, lo], 0), rhs[...])
    res[...] = both[:128] + both[128:]
    for r in range(8):
        for half in range(2):
            rows_out[half * 8 : half * 8 + 8, r * 128 : (r + 1) * 128] = res[pl.ds(half * 64 + r, 8, stride=8), :]
    store_e().wait()
    for x in range(8):
        store_t(x).wait()


def solution(mesh):
    n_gx, n_gy = mesh.shape["gx"], mesh.shape["gy"]
    vmem = pl.BlockSpec(memory_space=pltpu.VMEM)
    hbm = pl.BlockSpec(memory_space=pltpu.HBM)
    dma = pltpu.SemaphoreType.DMA

    def in_hbm(x):
        return pltpu.with_memory_space_constraint(x, pltpu.HBM)

    def tiles(*shape):
        return pltpu.VMEM((*shape, 8, 128), F32)

    def local(enthalpy_start, tangent_start, labels, curve_parameters, pixel_cells, row_slot):
        mid, rcv = pl.pallas_call(
            functools.partial(kernel, n_gx, n_gy),
            out_shape=[
                jax.ShapeDtypeStruct((8, 136, 128), F32),
                jax.ShapeDtypeStruct((5, 128, 128), F32),
            ],
            in_specs=[hbm] * 6,
            out_specs=[vmem, vmem],
            scratch_shapes=[
                pltpu.VMEM((64, 128), F32),
                pltpu.VMEM((64, 128), jnp.int32),
                pltpu.VMEM((8, 128), jnp.int32),
                pltpu.VMEM((8, 128), jnp.int32),
                pltpu.SMEM((COEF,), F32),
                pltpu.VMEM((8, 144, 128), F32),
                pltpu.VMEM((2, DEEP, 144, 128), F32),
                pltpu.VMEM((2, DEEP, 136, 128), F32),
                pltpu.VMEM((ROUNDS, 2, 40, 128), F32),
                pltpu.VMEM((ROUNDS, 3, 2, 40, 128), F32),
                tiles((COEF + 2) * STRIP),
                tiles(2 * ALL),
                tiles(ALL),
                tiles(4 * ALL),
                tiles(3 * ALL),
                tiles(ROUNDS * DEEP * ALL),
                tiles(ROUNDS * DEEP * COEF * ALL),
                pltpu.VMEM((128, 1024), BF16),
                pltpu.VMEM((8, MOST, 128), F32),
                pltpu.VMEM((128, 1024), BF16),
                pltpu.VMEM((256, 1024), BF16),
                tiles(COEF + 1),
                pltpu.VMEM((5, 128, 128), F32),
                dma((13,)),
                dma((ROUNDS, 5, 2)), dma((ROUNDS, 5, 2)),
                dma((ROUNDS, 3, 3, 2)), dma((ROUNDS, 3, 3, 2)),
                pltpu.SemaphoreType.REGULAR((3,)), dma, dma, dma,
            ],
            compiler_params=pltpu.CompilerParams(
                collective_id=0, has_side_effects=True, vmem_limit_bytes=40 * 2**20
            ),
            name="steps",
        )(
            in_hbm(enthalpy_start.reshape(64, 128)), in_hbm(tangent_start.reshape(128, 8, 128)),
            in_hbm(labels.reshape(64, 128)), in_hbm(curve_parameters),
            in_hbm(pixel_cells.reshape(8, 128)), in_hbm(row_slot.reshape(8, 128)),
        )
        e_end, t_end, rows = pl.pallas_call(
            finish,
            out_shape=[
                jax.ShapeDtypeStruct((64, 128), F32),
                jax.ShapeDtypeStruct((128, 8, 128), F32),
                jax.ShapeDtypeStruct((COEF, 1024), F32),
            ],
            in_specs=[vmem, vmem],
            out_specs=[hbm, hbm, vmem],
            scratch_shapes=[
                pltpu.VMEM((64, 128), F32),
                pltpu.VMEM((128, 4096), F32),
                pltpu.VMEM((128, 4096), BF16),
                pltpu.VMEM((128, 128), F32),
                dma((9,)),
            ],
            compiler_params=pltpu.CompilerParams(vmem_limit_bytes=40 * 2**20),
            name="finish",
        )(mid, rcv)
        return e_end.reshape(8, 8, 128), t_end.reshape(COEF, 8, 8, 128), rows

    in_specs = (
        P(None, "gx", "gy"),
        P(None, None, "gx", "gy"),
        P(None, "gx", "gy"),
        P(),
        P(("gx", "gy")),
        P(("gx", "gy")),
    )
    out_specs = (P(None, "gx", "gy"), P(None, None, "gx", "gy"), P(None, ("gx", "gy")))
    return jax.shard_map(local, mesh=mesh, in_specs=in_specs, out_specs=out_specs, check_vma=False)
```

```python
import functools
import math

import jax
import jax.numpy as jnp
from jax import lax
from jax.experimental import pallas as pl
from jax.experimental.pallas import tpu as pltpu
from jax.sharding import PartitionSpec as P

COEF = 16
RATE = 0.15
WIDTH = 0.3
ROOT = math.sqrt(math.log2(math.e))
KNOTS = [-2.0 + 0.25 * (j + 0.5) for j in range(COEF)]

DEEP = 4
ROUNDS = 2
MAIN = 16
STRIP = 4
ALL = MAIN + STRIP
ENTH = COEF
MOST = 32
GROUPS = ((0, 1, 2, 3),)
MESH = pl.DeviceIdType.MESH
F32 = jnp.float32
BF16 = jnp.bfloat16


def lanes():
    return lax.broadcasted_iota(jnp.int32, (8, 128), 1)


def turn(v, shift, axis):
    shift = shift % v.shape[axis]
    return v if shift == 0 else pltpu.roll(v, shift, axis)


def place(v, mask, piece):
    return piece if v is None else jnp.where(mask, piece, v)


def own_strips(rows):
    lane = lanes()
    out = []
    for g in range(STRIP):
        v = None
        for c in (1, 2):
            row = rows[4 * (c - 1) + g]
            v = place(v, lane // 16 == c, turn(row, 16 * c + 4, 1))
            v = place(v, lane // 16 == 4 + c, turn(row, 64 + 16 * c - 116, 1))
        out.append(v)
    return out


def pack_edges(strips, it, last, first):
    lane = lanes()
    for g in range(STRIP):
        here = (lane // 32 == g) & (lane % 16 // 4 == it)
        last = place(last, here, turn(strips[g], 32 * g + 4 * it - 88, 1))
        first = place(first, here, turn(strips[g], 32 * g + 4 * it - 20, 1))
    return last, first


def widen(edges):
    lane = lanes()
    low, own, high = edges
    out = []
    for h in range(2):
        v = None
        for g in (2 * h, 2 * h + 1):
            base = 64 * (g % 2)
            v = place(v, (lane >= base + 16) & (lane < base + 48), turn(own, base + 16 - 32 * g, 1))
            v = place(v, lane // 16 == base // 16, turn(low, base - 16 - 32 * g, 1))
            v = place(v, lane // 16 == base // 16 + 3, turn(high, base + 48 - 32 * g, 1))
        out.append(v)
    return out


def full_strips(own, low, high, before, after, it):
    lane = lanes()
    block, inside = lane // 16, lane % 16
    out = []
    for g in range(STRIP):
        v = own[g]
        v = place(v, block == 0, turn(low[g], 4, 1))
        v = place(v, block == 3, turn(high[g], 52, 1))
        v = place(v, block == 4, turn(low[g], -52, 1))
        v = place(v, block == 7, turn(high[g], -4, 1))
        at = 64 * (g % 2) + 4 * it
        v = place(v, (block < 4) & (inside < 4), turn(before[g // 2], -at, 1))
        v = place(v, (block >= 4) & (inside >= 12), turn(after[g // 2], 76 - at, 1))
        out.append(v)
    return out


def merge(state):
    lane = lanes()
    out = []
    for x in range(8):
        c, g = 1 + x // 4, x % 4
        v = jnp.where(lane < 4, turn(state[MAIN + g], -(16 * c + 4), 1), state[x + DEEP])
        out.append(jnp.where(lane >= 124, turn(state[MAIN + g], 124 - (72 + 16 * c), 1), v))
    return out


def advance(step, fields, load, store, temp, wx, wy, wz):
    def temps(i):
        olds = [load(k, i) for k in fields]
        return olds, [temp(k, i, v) for k, v in zip(fields, olds)]

    def across(i, ts, nexts):
        w = wx(i)
        return [w * (b - a) for a, b in zip(ts, nexts)]

    def update(i, olds, ts, fluxes, below):
        y, z = wy(i), wz(i)
        for k, old, t, flux, under in zip(fields, olds, ts, fluxes, below):
            fy = y * (turn(t, -1, 1) - t)
            fz = z * (turn(t, -1, 0) - t)
            store(k, i, old + ((flux - under) + ((fy - turn(fy, 1, 1)) + (fz - turn(fz, 1, 0)))))

    both = [temps(i) for i in range(MAIN, ALL)]
    ts = [t for _, t in both]
    ts.append([turn(t, -16, 1) for t in ts[0]])
    fluxes = [across(MAIN + g, ts[g], ts[g + 1]) for g in range(STRIP)]
    first = [turn(f, 16, 1) for f in fluxes[-1]]
    for g in range(STRIP):
        update(MAIN + g, *both[g], fluxes[g], fluxes[g - 1] if g > 0 else first)
    lo, hi = step, MAIN - step
    old, t = temps(lo)
    old_next, t_next = temps(lo + 1)
    flux = across(lo, t, t_next)
    for i in range(lo + 1, hi - 1):
        old, t = old_next, t_next
        old_next, t_next = temps(i + 1)
        below, flux = flux, across(i, t, t_next)
        update(i, old, t, flux, below)


def nt(a, b):
    return lax.dot_general(a, b, (((1,), (1,)), ((), ())), preferred_element_type=F32)


def hot(rows, row):
    return jnp.where(rows == row, 1.0, 0.0)


def kernel(
    n_gx, n_gy,
    e_ref, t_ref, lab_ref, coef_ref, cell_ref, slot_ref,
    mid, rcv,
    e_in, lab_in, cell_in, slot_in, coef_in, own, hx0, hx1, pk, hp, own_st, est, tst, fst, wst, sl, bump,
    a_ref, atk, tab, m_ref, top_st, snd,
    in_sem, x_send, x_recv, p_send, p_recv, near_sem, local_sem, all_send, all_recv,
):
    n = n_gx * n_gy
    gx, gy = lax.axis_index("gx"), lax.axis_index("gy")
    me = gx * n_gy + gy

    def at(dx, dy):
        return lax.rem(gx + dx + n_gx, n_gx), lax.rem(gy + dy + n_gy, n_gy)

    corners = [(dx, dy) for dx in (-1, 1, 0) for dy in (-1, 1)]
    around = corners + [(-1, 0), (1, 0)]
    rounds = [around, [(2 * dx, 2 * dy) for dx, dy in around], [(-4, 0), (4, 0)]]

    def greet(k):
        for dx, dy in rounds[k]:
            pl.semaphore_signal(near_sem.at[k], inc=1, device_id=at(dx, dy), device_id_type=MESH)

    def greeted(k):
        pl.semaphore_wait(near_sem.at[k], len(rounds[k]))

    barrier = pltpu.get_barrier_semaphore()
    for dx, dy in around:
        pl.semaphore_signal(barrier, inc=1, device_id=at(dx, dy), device_id_type=MESH)

    def load_e():
        return pltpu.make_async_copy(e_ref, e_in, in_sem.at[8])

    def load_lab():
        return pltpu.make_async_copy(lab_ref, lab_in, in_sem.at[9])

    def load_t(x):
        return pltpu.make_async_copy(t_ref.at[:, x, :], own.at[x, pl.ds(0, 128), :], in_sem.at[x])

    def load_cell():
        return pltpu.make_async_copy(cell_ref, cell_in, in_sem.at[10])

    def load_slot():
        return pltpu.make_async_copy(slot_ref, slot_in, in_sem.at[11])

    def load_coef():
        return pltpu.make_async_copy(coef_ref, coef_in, in_sem.at[12])

    load_e().start()
    load_lab().start()
    for x in range(8):
        load_t(x).start()
    load_cell().start()
    load_slot().start()
    load_coef().start()
    load_e().wait()
    load_lab().wait()
    pair = [[], []]
    for x in range(8):
        pair[0].append(e_in[pl.ds(x, 8, stride=8), :])
        pair[1].append(jnp.where(lab_in[pl.ds(x, 8, stride=8), :] == 1, 1.0, 0.0))
        for k in range(2):
            own[x, (ENTH + k) * 8 : (ENTH + k + 1) * 8, :] = pair[k][x]

    halos = (hx0, hx1)

    def send_x(r, q, d):
        part = pl.ds(q * 32, 32) if not isinstance(q, int) or q < 4 else pl.ds(128, 16 if r == 0 else 8)
        source = own if r == 0 else mid
        return pltpu.make_async_remote_copy(
            source.at[pl.ds(DEEP - DEEP * d, DEEP), part, :], halos[r].at[d, :, part, :],
            x_send.at[r, q, d], x_recv.at[r, q, d], device_id=at(1 - 2 * d, 0), device_id_type=MESH,
        )

    def send_p(r, group, dx, dy):
        part = pl.ds(32, 8) if group == 2 else pl.ds(0, 32) if r == 0 else pl.ds(group * 16, 16)
        side = 0 if dy == 1 else 1
        return pltpu.make_async_remote_copy(
            pk.at[r, side, part], hp.at[r, 1 - dx, side, part],
            p_send.at[r, group, dx + 1, side], p_recv.at[r, group, 1 - dx, side],
            device_id=at(dx, dy), device_id_type=MESH,
        )

    def store_pack(r, q, last, first):
        to = pl.ds(pl.multiple_of(q * 8, 8), 8)
        pk[r, 0, to, :] = last
        pk[r, 1, to, :] = first

    def store_strips(item, strips):
        for g in range(STRIP):
            own_st[item * STRIP + g] = strips[g]

    last = first = None
    for k in range(2):
        strips = own_strips(pair[k])
        store_strips(ENTH + k, strips)
        last, first = pack_edges(strips, k, last, first)
    store_pack(0, 4, last, first)

    pl.semaphore_wait(barrier, len(around))
    for dx, dy in corners:
        send_p(0, 2, dx, dy).start()
    for d in range(2):
        send_x(0, 4, d).start()
    for x in range(8):
        load_t(x).wait()
    for d in range(2):
        send_x(0, 0, d).start()

    def own_rows(ref, item):
        part = pl.ds(pl.multiple_of(item * 8, 8), 8)
        return [ref[x, part, :] for x in range(8)]

    def pack_quad(q, _):
        last = first = None
        for it in range(4):
            strips = own_strips(own_rows(own, q * 4 + it))
            store_strips(q * 4 + it, strips)
            last, first = pack_edges(strips, it, last, first)
        store_pack(0, q, last, first)
        return 0

    lax.fori_loop(0, 4, pack_quad, 0)
    for dx, dy in corners:
        send_p(0, 0, dx, dy).start()
    for q in range(1, 4):
        for d in range(2):
            send_x(0, q, d).start()

    greet(0)

    tall = lax.broadcasted_iota(jnp.int32, (128, 128), 0).astype(F32)
    wide = lax.broadcasted_iota(jnp.int32, (128, 128), 1).astype(F32)
    eight = lax.broadcasted_iota(jnp.int32, (8, 128), 0).astype(F32)
    load_cell().wait()
    load_slot().wait()
    load_coef().wait()
    cell, slot = cell_in[...], slot_in[...]
    owner = (slot // 1024).astype(F32)
    row = slot % 1024
    row_hi, row_lo = (row // 128 + 1).astype(F32), (row % 128).astype(F32)
    cell_x, cell_y = (cell // 128).astype(F32), (cell % 128).astype(F32)
    by_cell = jnp.zeros((24, 128), F32)
    for b in range(8):
        here = hot(eight, cell_x[b : b + 1])
        left = jnp.concatenate([here * w[b : b + 1] for w in (owner, row_hi, row_lo)], 0)
        by_cell = by_cell + nt(left.astype(BF16), hot(tall, cell_y[b : b + 1]).astype(BF16))
    owner, row_hi, row_lo = by_cell[0:8], by_cell[8:16], by_cell[16:24]
    earlier = jnp.where(tall < wide, 1.0, 0.0).astype(BF16)
    ones = jnp.ones((128, 128), BF16)
    seen = jnp.zeros((128, 128), F32)
    slot_k = lax.broadcasted_iota(jnp.int32, (MOST, 128), 0).astype(F32)
    for x in range(8):
        cols = slice(x * 128, (x + 1) * 128)
        mine = hot(tall, owner[x : x + 1])
        mine_b = mine.astype(BF16)
        a_ref[:, cols] = mine_b
        count = jnp.dot(mine_b, earlier, preferred_element_type=F32) + jnp.dot(
            seen.astype(BF16), ones, preferred_element_type=F32
        )
        seen = seen + mine
        at_k = hot(slot_k, jnp.sum(mine * count, axis=0, keepdims=True))
        atk[x] = at_k
        tab[0:MOST, cols] = (at_k * row_hi[x : x + 1]).astype(BF16)
        tab[MOST : 2 * MOST, cols] = (at_k * row_lo[x : x + 1]).astype(BF16)
        tab[2 * MOST : 4 * MOST, cols] = jnp.zeros((2 * MOST, 128), BF16)
    snd[4] = nt(a_ref[...], tab[...])

    def shape_row(r, s, i):
        e = est[i]
        p = est[ALL + i] > 0
        scaled = jnp.where(p, e, 100.0) * (ROOT / WIDTH)
        total = jnp.zeros((8, 128), F32)
        slope = jnp.zeros((8, 128), F32)
        for j in range(COEF):
            v = scaled - KNOTS[j] * (ROOT / WIDTH)
            b = jnp.exp2(-(v * v))
            bump[((r * DEEP + s) * COEF + j) * ALL + i] = b
            cb = coef_in[j] * b
            total = total + cb
            slope = slope + v * cb
        half = jnp.where(p, 1.0, 0.5)
        tst[i] = half * e + total
        sl[(r * DEEP + s) * ALL + i] = half - (2.0 / (WIDTH * ROOT)) * slope

    def shape_rows(r, s, lo, hi):
        for i in range(lo, hi):
            shape_row(r, s, i)

    def halo_rows(r, d, item):
        part = pl.ds(pl.multiple_of(item * 8, 8), 8)
        return [halos[r][d, x, part, :] for x in range(DEEP)]

    def wide_edges(r, q):
        part = pl.ds(pl.multiple_of(q * 8, 8), 8)
        return [widen([hp[r, k, side, part, :] for k in range(3)]) for side in range(2)]

    def all_rows(r, item, wide, it):
        low, high = halo_rows(r, 0, item), halo_rows(r, 1, item)
        main = low + own_rows(own if r == 0 else mid, item) + high
        strips = [own_st[item * STRIP + g] for g in range(STRIP)]
        return main + full_strips(strips, low, high, *wide, it)

    def wait_e(r):
        for d in range(2):
            send_x(r, 4, d).wait()
        for dx, dy in corners:
            send_p(r, 2, dx, dy).wait()

    for x in range(8):
        est[DEEP + x] = own[x, ENTH * 8 : ENTH * 8 + 8, :]
        est[ALL + DEEP + x] = own[x, (ENTH + 1) * 8 : (ENTH + 2) * 8, :]
    shape_rows(0, 0, DEEP, MAIN - DEEP)
    wait_e(0)
    pcm = all_rows(0, ENTH + 1, wide_edges(0, 4), 1)
    for i in range(ALL):
        est[ALL + i] = pcm[i]

    lane = lanes()
    block, inside = lane // 16, lane % 16
    layer = lax.broadcasted_iota(jnp.int32, (8, 128), 0)
    open_x0 = jnp.where(gx == 0, 0.0, 1.0)
    open_x1 = jnp.where(gx == n_gx - 1, 0.0, 1.0)
    open_y0 = jnp.where(gy == 0, 0.0, 1.0)
    open_y1 = jnp.where(gy == n_gy - 1, 0.0, 1.0)
    cond = [1.0 - 0.5 * p for p in pcm]

    def face(a, b):
        return (2.0 * RATE) * a * b / (a + b)

    edge_y = jnp.where((block < 4) & (inside == 3), open_y0, 1.0)
    edge_y = jnp.where((block >= 4) & (inside == 11), open_y1, edge_y)
    edge_x = jnp.where((block == 0) | (block == 4), open_x0, 1.0)
    edge_x = jnp.where((block == 2) | (block == 6), open_x1, edge_x)
    for i in range(ALL):
        c = cond[i]
        if i == MAIN - 1:
            up = c
        elif i == ALL - 1:
            up = turn(cond[MAIN], -16, 1)
        else:
            up = cond[i + 1]
        wx = face(c, up)
        if i == 3:
            wx = wx * open_x0
        if i == 11:
            wx = wx * open_x1
        if i == ALL - 1:
            wx = wx * edge_x
        wst[i] = wx
        wy = face(c, turn(c, -1, 1))
        wst[ALL + i] = wy * edge_y if i >= MAIN else wy
        wst[2 * ALL + i] = jnp.where(layer == 7, 0.0, face(c, turn(c, -1, 0)))

    weights = (lambda i: wst[i], lambda i: wst[ALL + i], lambda i: wst[2 * ALL + i])

    def keep_e(k, i, v):
        est[i] = v

    def enthalpy(r):
        start = all_rows(r, ENTH, wide_edges(r, 4), 0)
        for i in range(ALL):
            est[i] = start[i]
        for s in range(DEEP):
            if r == 0 and s == 0:
                shape_rows(r, s, 0, DEEP)
                shape_rows(r, s, MAIN - DEEP, ALL)
            else:
                shape_rows(r, s, s, MAIN - s)
                shape_rows(r, s, MAIN, ALL)
            advance(s, [0], lambda k, i: est[i], keep_e, lambda k, i, v: tst[i], *weights)
        state = [est[i] for i in range(ALL)]
        done = merge(state)
        for x in range(8):
            mid[x, ENTH * 8 : ENTH * 8 + 8, :] = done[x]
        if r == 0:
            store_strips(ENTH, state[MAIN:])
            last, first = pack_edges(state[MAIN:], 0, None, None)
            store_pack(1, 4, last, first)

    def keep_t(k, i, v):
        fst[k * ALL + i] = v

    def tangents(r, q):
        last = first = None
        wide = wide_edges(r, q)
        for its in GROUPS:
            for it in its:
                for i, v in enumerate(all_rows(r, q * 4 + it, wide, it)):
                    fst[it * ALL + i] = v
            for s in range(DEEP):
                def temp(k, i, v, s=s):
                    return sl[(r * DEEP + s) * ALL + i] * v + bump[((r * DEEP + s) * COEF + q * 4 + k) * ALL + i]

                advance(s, its, lambda k, i: fst[k * ALL + i], keep_t, temp, *weights)
            for it in its:
                j = q * 4 + it
                state = [fst[it * ALL + i] for i in range(ALL)]
                done = merge(state)
                part = pl.ds(pl.multiple_of(j * 8, 8), 8)
                for x in range(8):
                    mid[x, part, :] = done[x]
                if r == 0:
                    store_strips(j, state[MAIN:])
                    last, first = pack_edges(state[MAIN:], it, last, first)
        if r == 0:
            store_pack(1, q, last, first)

    enthalpy(0)
    greeted(0)
    greet(1)
    for dx, dy in corners:
        send_p(1, 2, dx, dy).start()
    for d in range(2):
        send_x(1, 4, d).start()
    for dx, dy in corners:
        send_p(0, 0, dx, dy).wait()

    def first_round(q, _):
        for d in range(2):
            send_x(0, q, d).wait()
        tangents(0, q)
        for group in range(2):
            @pl.when(q == 2 * group + 1)
            def _():
                for dx, dy in corners:
                    send_p(1, group, dx, dy).start()
        for d in range(2):
            send_x(1, q, d).start()
        return 0

    lax.fori_loop(0, 4, first_round, 0)
    greeted(1)
    greet(2)
    wait_e(1)
    enthalpy(1)

    def top(item):
        v = jnp.broadcast_to(mid[0, pl.ds(item * 8 + 7, 1), :], (8, 128))
        for x in range(1, 8):
            v = jnp.where(eight == x, mid[x, pl.ds(item * 8 + 7, 1), :], v)
        return v

    p7 = jnp.where(lab_in[56:64, :] == 1, 1.0, 0.0) > 0
    scaled = jnp.where(p7, top(ENTH), 100.0) * (ROOT / WIDTH)
    slope = jnp.zeros((8, 128), F32)
    for j in range(COEF):
        v = scaled - KNOTS[j] * (ROOT / WIDTH)
        b = jnp.exp2(-(v * v))
        top_st[j] = b
        slope = slope + v * (coef_in[j] * b)
    top_st[COEF] = jnp.where(p7, 1.0, 0.5) - (2.0 / (WIDTH * ROOT)) * slope

    def pack_rows(q):
        for it in range(4):
            f = q * 4 + it
            val = top_st[COEF] * top(f) + top_st[f]
            hi = val.astype(BF16).astype(F32)
            lo = val - hi
            for x in range(8):
                cols = slice(x * 128, (x + 1) * 128)
                at_k = atk[x]
                m_ref[it * MOST : (it + 1) * MOST, cols] = (at_k * hi[x : x + 1]).astype(BF16)
                m_ref[128 + it * MOST : 128 + (it + 1) * MOST, cols] = (at_k * lo[x : x + 1]).astype(BF16)
        both = nt(a_ref[...], m_ref[...])
        snd[q] = both[:, :128] + both[:, 128:]

    def second_round(q, _):
        for group in range(2):
            @pl.when(q == 2 * group)
            def _():
                for dx, dy in corners:
                    send_p(1, group, dx, dy).wait()
        for d in range(2):
            send_x(1, q, d).wait()
        tangents(1, q)
        pack_rows(q)
        return 0

    lax.fori_loop(0, 4, second_round, 0)

    greeted(2)
    mine = pl.ds(me, 1)
    keep = pltpu.make_async_copy(snd.at[:, mine, :], rcv.at[:, mine, :], local_sem)
    keep.start()

    def send_rows(i, _):
        t = lax.rem(me + i, n)
        pltpu.make_async_remote_copy(
            snd.at[:, pl.ds(t, 1), :], rcv.at[:, mine, :], all_send, all_recv,
            device_id=(t // n_gy, lax.rem(t, n_gy)), device_id_type=MESH,
        ).start()
        return 0

    lax.fori_loop(1, n, send_rows, 0)
    keep.wait()
    rest = pl.ds(0, n - 1)
    pltpu.make_async_remote_copy(
        snd.at[:, rest, :], rcv.at[:, rest, :], all_send, all_recv, device_id=at(1, 0), device_id_type=MESH
    ).wait()


def finish(mid, rcv, e_out, t_out, rows_out, e_tile, lhs, rhs, res, sem):
    def store_t(x):
        return pltpu.make_async_copy(mid.at[x, pl.ds(0, 128), :], t_out.at[:, x, :], sem.at[x])

    def store_e():
        return pltpu.make_async_copy(e_tile, e_out, sem.at[8])

    for x in range(8):
        store_t(x).start()
    for x in range(8):
        e_tile[pl.ds(x, 8, stride=8), :] = mid[x, ENTH * 8 : ENTH * 8 + 8, :]
    store_e().start()

    tall = lax.broadcasted_iota(jnp.int32, (128, 128), 0).astype(F32)
    eight = lax.broadcasted_iota(jnp.int32, (8, 128), 0).astype(F32)
    where = rcv[4].T
    vals = [rcv[g].T for g in range(4)]
    for k in range(MOST):
        cols = slice(k * 128, (k + 1) * 128)
        rhs[:, cols] = hot(tall, where[MOST + k : MOST + k + 1]).astype(BF16)
        at_hi = hot(eight + 1.0, where[k : k + 1])
        for f in range(COEF):
            at_f = (f % 4) * MOST + k
            lhs[f * 8 : f * 8 + 8, cols] = at_hi * vals[f // 4][at_f : at_f + 1]
    whole = lhs[...]
    hi = whole.astype(BF16)
    lo = (whole - hi.astype(F32)).astype(BF16)
    both = nt(jnp.concatenate([hi, lo], 0), rhs[...])
    res[...] = both[:128] + both[128:]
    for r in range(8):
        for half in range(2):
            rows_out[half * 8 : half * 8 + 8, r * 128 : (r + 1) * 128] = res[pl.ds(half * 64 + r, 8, stride=8), :]
    store_e().wait()
    for x in range(8):
        store_t(x).wait()


def solution(mesh):
    n_gx, n_gy = mesh.shape["gx"], mesh.shape["gy"]
    vmem = pl.BlockSpec(memory_space=pltpu.VMEM)
    hbm = pl.BlockSpec(memory_space=pltpu.HBM)
    dma = pltpu.SemaphoreType.DMA

    def in_hbm(x):
        return pltpu.with_memory_space_constraint(x, pltpu.HBM)

    def tiles(*shape):
        return pltpu.VMEM((*shape, 8, 128), F32)

    def local(enthalpy_start, tangent_start, labels, curve_parameters, pixel_cells, row_slot):
        mid, rcv = pl.pallas_call(
            functools.partial(kernel, n_gx, n_gy),
            out_shape=[
                jax.ShapeDtypeStruct((8, 136, 128), F32),
                jax.ShapeDtypeStruct((5, 128, 128), F32),
            ],
            in_specs=[hbm] * 6,
            out_specs=[vmem, vmem],
            scratch_shapes=[
                pltpu.VMEM((64, 128), F32),
                pltpu.VMEM((64, 128), jnp.int32),
                pltpu.VMEM((8, 128), jnp.int32),
                pltpu.VMEM((8, 128), jnp.int32),
                pltpu.SMEM((COEF,), F32),
                pltpu.VMEM((8, 144, 128), F32),
                pltpu.VMEM((2, DEEP, 144, 128), F32),
                pltpu.VMEM((2, DEEP, 136, 128), F32),
                pltpu.VMEM((ROUNDS, 2, 40, 128), F32),
                pltpu.VMEM((ROUNDS, 3, 2, 40, 128), F32),
                tiles((COEF + 2) * STRIP),
                tiles(2 * ALL),
                tiles(ALL),
                tiles(4 * ALL),
                tiles(3 * ALL),
                tiles(ROUNDS * DEEP * ALL),
                tiles(ROUNDS * DEEP * COEF * ALL),
                pltpu.VMEM((128, 1024), BF16),
                pltpu.VMEM((8, MOST, 128), F32),
                pltpu.VMEM((128, 1024), BF16),
                pltpu.VMEM((256, 1024), BF16),
                tiles(COEF + 1),
                pltpu.VMEM((5, 128, 128), F32),
                dma((13,)),
                dma((ROUNDS, 5, 2)), dma((ROUNDS, 5, 2)),
                dma((ROUNDS, 3, 3, 2)), dma((ROUNDS, 3, 3, 2)),
                pltpu.SemaphoreType.REGULAR((3,)), dma, dma, dma,
            ],
            compiler_params=pltpu.CompilerParams(
                collective_id=0, has_side_effects=True, vmem_limit_bytes=40 * 2**20
            ),
            name="steps",
        )(
            in_hbm(enthalpy_start.reshape(64, 128)), in_hbm(tangent_start.reshape(128, 8, 128)),
            in_hbm(labels.reshape(64, 128)), in_hbm(curve_parameters),
            in_hbm(pixel_cells.reshape(8, 128)), in_hbm(row_slot.reshape(8, 128)),
        )
        e_end, t_end, rows = pl.pallas_call(
            finish,
            out_shape=[
                jax.ShapeDtypeStruct((64, 128), F32),
                jax.ShapeDtypeStruct((128, 8, 128), F32),
                jax.ShapeDtypeStruct((COEF, 1024), F32),
            ],
            in_specs=[vmem, vmem],
            out_specs=[hbm, hbm, vmem],
            scratch_shapes=[
                pltpu.VMEM((64, 128), F32),
                pltpu.VMEM((128, 4096), F32),
                pltpu.VMEM((128, 4096), BF16),
                pltpu.VMEM((128, 128), F32),
                dma((9,)),
            ],
            compiler_params=pltpu.CompilerParams(vmem_limit_bytes=40 * 2**20),
            name="finish",
        )(mid, rcv)
        return e_end.reshape(8, 8, 128), t_end.reshape(COEF, 8, 8, 128), rows

    in_specs = (
        P(None, "gx", "gy"),
        P(None, None, "gx", "gy"),
        P(None, "gx", "gy"),
        P(),
        P(("gx", "gy")),
        P(("gx", "gy")),
    )
    out_specs = (P(None, "gx", "gy"), P(None, None, "gx", "gy"), P(None, ("gx", "gy")))
    return jax.shard_map(local, mesh=mesh, in_specs=in_specs, out_specs=out_specs, check_vma=False)
```
